32 devices in a mesh: dp: 8 (over z, y), mp: 2 (over core), side: 2 (over x).
Axes of the slice: x: 2, y: 2, z: 4, core: 2. Of those that a mesh axis runs over, the one named last changes fastest.
Arguments:
- tokens: bfloat16 [2048, 3072], P('dp', 'mp'), may hold values from -6 to 6
- up_weight: bfloat16 [2, 3072, 6144], P('side', 'dp', 'mp'), may hold values from -0.109375 to 0.109375
- down_weight: bfloat16 [2, 6144, 3072], P('side', 'mp', 'dp'), may hold values from -0.078125 to 0.078125
- mod_table: float32 [2, 50, 3, 3072], P('side'), may hold values from -3 to 3
- timesteps: int32 [8], P('dp'), may hold values from 0 to 49
- valid_counts: int32 [8], replicated, may hold values from 64 to 256, as said below
Outputs:
- block_out: bfloat16 [2, 2048, 3072], P('side', 'dp', 'mp')
- up_grads: float32 [3072, 6144], P(('dp', 'side'), 'mp')
- down_grads: float32 [6144, 3072], P('mp', ('dp', 'side'))
The draws below stay inside these ranges and needn't reach their ends.
Inputs may be any that keep to these rules, and one draw needn't show every extreme that they name: `valid_counts`: every image has at least 64 valid tokens, and in every draw some image has all 256 valid.
All inputs are finite; a program needn't handle non-finite values.
Results may differ from the reference program's by a relative error of at most 0.018.
Values may be sent and summed in bfloat16 or wider, within the bound.
No kernel may reach another device: no remote copies, remote signals or barrier semaphores. Data moves between devices by JAX's collectives and lax.ppermute only.
A program may use at most 128 MiB of HBM per device.

```python
import jax
import jax.numpy as jnp
from jax import lax

D = 3072
FFW = 6144
STEPS = 50
SEQ = 256
SAMPLES = 8
TOKENS = 2048
N_DP = 8


def draw_valid_counts(key, part):
    draw_key = jax.random.fold_in(key, 11)
    pick_key = jax.random.fold_in(key, 23)
    counts = jax.random.randint(draw_key, (SAMPLES,), SEQ // 4, SEQ + 1)
    chosen = jax.random.randint(pick_key, (), 0, SAMPLES)
    return jnp.where(jnp.arange(SAMPLES) == chosen, SEQ, counts).astype(jnp.int32)


def set_ends(array, own_key, low, largest):
    place = [jax.random.randint(jax.random.fold_in(own_key, axis), (), 0, length) for axis, length in enumerate(array.shape)]
    widest = array.shape.index(max(array.shape))
    next_to = place[:widest] + [(place[widest] + 1) % array.shape[widest]] + place[widest + 1:]
    return array.at[tuple(place)].set(low).at[tuple(next_to)].set(largest)


def strengthened(entries, own_key, source, target, parts, factor):
    def block_of(dim):
        return (jnp.arange(entries.shape[dim]) // (entries.shape[dim] // parts)).reshape((-1,) + (1,) * (entries.ndim - 1 - dim))

    one_side = jax.random.permutation(own_key, parts)[block_of(target)]
    far = (block_of(target) + parts // 2) % parts
    return jnp.where((block_of(source) == one_side) | (block_of(source) == far), factor * entries, entries)


def level_of(key, shape, pieces, least, high):
    gain = 1.0
    for position, shards_of in pieces:
        steps = jax.random.uniform(jax.random.fold_in(jax.random.fold_in(key, 6), position), (shards_of,), jnp.float32, least / len(pieces), high / len(pieces))
        gain = gain * jnp.repeat(jnp.exp(steps), shape[position] // shards_of).reshape((-1,) + (1,) * (len(shape) - 1 - position))
    return gain


def bell_draw(key, extent, spread, limit, shards=(), kind=jnp.bfloat16):
    level = level_of(key, extent, shards, -0.22, 0.18) if shards else 1.0
    entries = jax.random.normal(key, extent, jnp.float32) * spread * level
    return jnp.minimum(jnp.maximum(entries, -limit), limit).astype(kind)


def bell_draw_with(own_key, dims, width, bound, split, heavy, kind=jnp.bfloat16):
    values = width * jax.random.normal(own_key, dims, jnp.float32)
    if split:
        values = values * level_of(own_key, dims, split, -0.22, 0.18)
    return jnp.clip(strengthened(values, jax.random.fold_in(own_key, 3), *heavy), -bound, bound).astype(kind)


def setup_inputs(seed: int = 0) -> dict:
    key_list = jax.random.split(jax.random.key(seed), 7)
    return {
        "tokens": bell_draw_with(key_list[0], (TOKENS, D), 1.0, 6.0, ((0, 8), (1, 2)), (0, 1, 8, 2.0)),
        "up_weight": bell_draw(key_list[1], (2, D, FFW), D ** -0.5, 0.109375, ((0, 2), (1, 8), (2, 2))),
        "down_weight": bell_draw(key_list[2], (2, FFW, D), FFW ** -0.5, 0.078125, ((0, 2), (1, 2), (2, 8))),
        "mod_table": bell_draw(key_list[3], (2, STEPS, 3, D), 0.5, 3.0, ((0, 2),), jnp.float32),
        "timesteps": set_ends(jax.random.randint(key_list[4], (SAMPLES,), 0, STEPS), jax.random.fold_in(key_list[4], 1), 0, STEPS - 1).astype(jnp.int32),
        "valid_counts": draw_valid_counts(jax.random.fold_in(key_list[6], 71), 0),
    }


def gelu_tanh(values):
    return jax.nn.gelu(values, approximate=True)

def block_forward(tokens, up_matrix, down_matrix, table, timesteps):
    wide = tokens.astype(jnp.float32).reshape(N_DP, SEQ, D)
    average = lax.optimization_barrier(jnp.mean(wide, axis=-1, keepdims=True))
    centred = wide - average
    variance = lax.optimization_barrier(jnp.mean(centred * centred, axis=-1, keepdims=True))
    scaled = centred * lax.rsqrt(variance + 1e-06)
    modulation = table[timesteps]
    normed = (scaled * (1.0 + modulation[:, 1:2]) + modulation[:, 0:1]).astype(jnp.bfloat16).reshape(TOKENS, D)
    hidden_pre = jnp.dot(normed, up_matrix, preferred_element_type=jnp.float32)
    hidden_act = gelu_tanh(hidden_pre).astype(jnp.bfloat16)
    mixed = jnp.dot(hidden_act, down_matrix, preferred_element_type=jnp.float32).reshape(N_DP, SEQ, D)
    gate_rows = modulation[:, 2:3]
    output = (wide + gate_rows * mixed).astype(jnp.bfloat16).reshape(TOKENS, D)
    return (normed, hidden_pre, hidden_act, gate_rows, output)

def rounded_sum(left, right):

    def accumulate(running, index):
        left_rows = lax.dynamic_slice_in_dim(left, (index * SEQ).astype(jnp.int32), SEQ, 0)
        right_rows = lax.dynamic_slice_in_dim(right, (index * SEQ).astype(jnp.int32), SEQ, 0)
        term = lax.dot_general(left_rows, right_rows, (((0,), (0,)), ((), ())), preferred_element_type=jnp.float32)
        term = lax.optimization_barrier(term.astype(jnp.bfloat16))
        return (running + term.astype(jnp.float32), None)
    start_value = jnp.zeros((left.shape[1], right.shape[1]), jnp.float32)
    result, unused = lax.scan(accumulate, start_value, jnp.arange(N_DP, dtype=jnp.int32))
    return result

def block_grads(normed, hidden_pre, hidden_act, gate_rows, own, other, down_matrix, valid_counts):
    positions = jnp.arange(SEQ, dtype=jnp.int32)
    valid_rows = (positions[None, :] < valid_counts[:, None]).astype(jnp.float32)[:, :, None]
    valid_total = jnp.sum(valid_counts).astype(jnp.float32)
    differ = (own.astype(jnp.float32) - other.astype(jnp.float32)).reshape(N_DP, SEQ, D)
    grad_out = (gate_rows * differ * valid_rows / jnp.sqrt(valid_total)).astype(jnp.bfloat16).reshape(TOKENS, D)
    grad_act = lax.dot_general(grad_out, down_matrix, (((1,), (1,)), ((), ())), preferred_element_type=jnp.float32)
    unused, pullback = jax.vjp(gelu_tanh, hidden_pre)
    grad_pre = pullback(grad_act)[0].astype(jnp.bfloat16)
    return (rounded_sum(normed, grad_pre), rounded_sum(hidden_act, grad_out))

def reference(tokens, up_weight, down_weight, mod_table, timesteps, valid_counts):
    teacher = block_forward(tokens, up_weight[0], down_weight[0], mod_table[0], timesteps)
    student = block_forward(tokens, up_weight[1], down_weight[1], mod_table[1], timesteps)
    student_up, student_down = block_grads(student[0], student[1], student[2], student[3], student[4], teacher[4], down_weight[1], valid_counts)
    block_out = jnp.stack([teacher[4], student[4]])
    return (block_out, student_up, student_down)
```

```python
import jax
import jax.numpy as jnp
from jax import lax
from jax.experimental import pallas as pl
from jax.experimental.pallas import tpu as pltpu
from jax.sharding import PartitionSpec as P

LANES = 128


def gelu_tanh(values):
    return jax.nn.gelu(values, approximate=True)


def product(left, right):
    return jnp.dot(left, right, preferred_element_type=jnp.float32)


def over_tokens(left, right):
    return lax.dot_general(left, right, (((0,), (0,)), ((), ())), preferred_element_type=jnp.float32)


def across(left, right):
    return lax.dot_general(left, right, (((1,), (1,)), ((), ())), preferred_element_type=jnp.float32)


def ring_order(count):
    return list(range(0, count, 2)) + list(range(1, count, 2))[::-1]


def ring_shift(x, by):
    order = ring_order(lax.axis_size("dp"))
    count = len(order)
    return lax.ppermute(x, "dp", [(order[p], order[(p + by) % count]) for p in range(count)])


def from_core(x, by):
    count = lax.axis_size("mp")
    return lax.ppermute(x, "mp", [((c + by) % count, c) for c in range(count)])


def ring_gather(x, sign):
    count = lax.axis_size("dp")
    found = [x] * count
    there = back = x
    for hop in range(1, count // 2 + 1):
        there = ring_shift(there, sign)
        found[(-sign * hop) % count] = there
        if hop <= (count - 1) // 2:
            back = ring_shift(back, -sign)
            found[(sign * hop) % count] = back
    return found


def ring_scatter(terms, sign):
    count = lax.axis_size("dp")
    total = terms[0]
    for way, hops in ((sign, count // 2), (-sign, (count - 1) // 2)):
        if hops:
            running = terms[(way * hops) % count]
            for hop in range(hops - 1, -1, -1):
                arrived = ring_shift(running.astype(jnp.bfloat16), way).astype(jnp.float32)
                if hop:
                    running = arrived + terms[(way * hop) % count]
                else:
                    total = total + arrived
    return total


def in_vmem(count):
    return [pl.BlockSpec(memory_space=pltpu.VMEM)] * count


def placed_along(axis, offsets, pieces, length):
    extent = pieces[0].shape[axis]
    shape = list(pieces[0].shape)
    shape[axis] = length
    if axis == 1 and extent % LANES:
        result = jnp.zeros(shape, pieces[0].dtype)
        for k, piece in enumerate(pieces):
            result = lax.dynamic_update_slice_in_dim(result, piece, offsets[k], axis)
        return result

    def kernel(offset_ref, *refs):
        for k, ref in enumerate(refs[:-1]):
            where = pl.ds(pl.multiple_of(offset_ref[k], extent), extent)
            if axis == 0:
                refs[-1][where, :] = ref[...]
            else:
                refs[-1][:, where] = ref[...]

    return pl.pallas_call(
        kernel,
        out_shape=jax.ShapeDtypeStruct(shape, pieces[0].dtype),
        in_specs=[pl.BlockSpec(memory_space=pltpu.SMEM)] + in_vmem(len(pieces)),
        out_specs=pl.BlockSpec(memory_space=pltpu.VMEM),
        compiler_params=pltpu.CompilerParams(vmem_limit_bytes=16 << 20),
        cost_estimate=pl.CostEstimate(flops=0, bytes_accessed=4 * length * pieces[0].size // extent, transcendentals=0),
        name="place",
    )(jnp.stack(offsets).astype(jnp.int32), *pieces)


def received(side, offsets, arrivals, width):
    rows, share = arrivals[0][0].shape
    rows //= 2
    if share % LANES:
        results = []
        for top in (0, rows):
            result = jnp.zeros((rows, width), jnp.float32)
            for k, pieces in enumerate(arrivals):
                piece = lax.select_n(side, *[piece[top : top + rows] for piece in pieces]).astype(jnp.float32)
                result = lax.dynamic_update_slice_in_dim(result, piece, offsets[k], 1)
            results.append(result)
        return results
    sides = len(arrivals[0])
    flat = [piece for pieces in arrivals for piece in pieces]

    def kernel(offset_ref, *refs):
        for k in range(len(arrivals)):
            where = pl.ds(pl.multiple_of(offset_ref[k], share), share)
            for to in range(sides):

                @pl.when(offset_ref[len(arrivals)] == to)
                def _():
                    piece = refs[k * sides + to]
                    for half in range(2):
                        refs[-2 + half][:, where] = piece[half * rows : half * rows + rows, :].astype(jnp.float32)

    return pl.pallas_call(
        kernel,
        out_shape=[jax.ShapeDtypeStruct((rows, width), jnp.float32)] * 2,
        in_specs=[pl.BlockSpec(memory_space=pltpu.SMEM)] + in_vmem(len(flat)),
        out_specs=in_vmem(2),
        compiler_params=pltpu.CompilerParams(vmem_limit_bytes=24 << 20),
        name="received",
    )(jnp.stack(offsets + [side]).astype(jnp.int32), *flat)


def partner(index, step, count):
    return index ^ step if count & (count - 1) == 0 else (step - index) % count


def shards(tokens, up_weight, down_weight, mod_table, timesteps, valid_counts):
    count, cores, sides = lax.axis_size("dp"), lax.axis_size("mp"), lax.axis_size("side")
    me, core, side = lax.axis_index("dp"), lax.axis_index("mp"), lax.axis_index("side")
    rows, width = tokens.shape
    pieces = 2 if width % (2 * LANES) == 0 and cores == 2 else 1
    part = width // pieces
    block, hidden = up_weight.shape[1:]
    share = hidden // count
    features = block * count
    first = core * width if cores == 2 else 0
    peers = [partner(me, step, count) for step in range(count)]
    feature_offsets = [(peer * block - first) % features for peer in peers]

    def sent(step, piece, to=None):
        pairs = [(i, partner(i, step, count)) for i in range(count)]
        if to is not None:
            pairs = [(i * sides + sides - 1, j * sides + to) for i, j in pairs]
        if all(i == j for i, j in pairs):
            return piece
        return lax.ppermute(piece, "dp" if to is None else ("dp", "side"), pairs)

    ups = [sent(k, lax.dynamic_slice_in_dim(up_weight[0], peers[k] * share, share, 1)) for k in range(count)]
    downs = [sent(k, lax.dynamic_slice_in_dim(down_weight[0], peers[k] * share, share, 0)) for k in range(count)]
    up = placed_along(0, feature_offsets, ups, features)
    down = placed_along(1, feature_offsets, downs, features)

    wide = tokens.astype(jnp.float32)
    own_mean = jnp.mean(wide, axis=-1, keepdims=True)
    own_spread = jnp.sum((wide - own_mean) ** 2, axis=-1, keepdims=True)
    moments = jnp.concatenate([own_mean, own_spread], axis=1)
    if cores == 2:
        all_moments = jnp.stack([moments, from_core(moments, 1)])
    else:
        all_moments = lax.all_gather(moments, "mp")
    average = jnp.mean(all_moments[:, :, :1], axis=0)
    spread = jnp.sum(all_moments[:, :, 1:] + width * (all_moments[:, :, :1] - average) ** 2, axis=0)
    scaled = (wide - average) * lax.rsqrt(spread / features + 1e-06)
    modulation = lax.dynamic_slice(
        mod_table[0], (timesteps[0], 0, core * width), (1, mod_table.shape[2], width)
    )[0]
    normed = (scaled * (1.0 + modulation[1]) + modulation[0]).astype(jnp.bfloat16)
    gate = modulation[2]

    def spread_out(piece, index):
        found = ring_gather(piece, 1 if index % 2 == 0 else -1)
        return [found, [from_core(x, 1) for x in found]] if cores == 2 else of_all_cores(found)

    def of_all_cores(found):
        everything = lax.all_gather(jnp.concatenate(found, axis=0), "mp")
        return [[everything[t]] for t in range(cores)]

    def at(t, c):
        start = t * width + c * part
        return slice(start, start + part)

    parts = [(t, c) for t in range(cores) for c in range(pieces)]

    def summed(found, weight, times):
        return jnp.concatenate(
            [sum(times(found[c][t][r], weight(t, c)) for t, c in parts) for r in range(len(found[0][0]))], axis=0
        )

    all_normed = [spread_out(normed[:, c * part : (c + 1) * part], c) for c in range(pieces)]
    hidden_pre = summed(all_normed, lambda t, c: up[at(t, c)], product)
    hidden_act = gelu_tanh(hidden_pre).astype(jnp.bfloat16)

    valid_col = (jnp.arange(rows, dtype=jnp.int32) < valid_counts[me]).astype(jnp.float32)[:, None]
    valid_total = jnp.sum(valid_counts).astype(jnp.float32)

    outs, all_grads = [], []
    for c in range(pieces):
        if cores == 2:
            away = product(hidden_act, down[:, at(1, c)]).astype(jnp.bfloat16)
            term = product(hidden_act, down[:, at(0, c)]) + from_core(away, 1).astype(jnp.float32)
        else:
            term = lax.psum_scatter(
                product(hidden_act, down).astype(jnp.bfloat16), "mp", scatter_dimension=1, tiled=True
            ).astype(jnp.float32)
        mixed = ring_scatter([term[r * rows : (r + 1) * rows] for r in range(count)], 1 if c % 2 == 0 else -1)
        own = slice(c * part, (c + 1) * part)
        out = (wide[:, own] + gate[own] * mixed).astype(jnp.bfloat16)
        other = lax.ppermute(out, "side", [(i, i + 1) for i in range(sides - 1)])
        differ = out.astype(jnp.float32) - other.astype(jnp.float32)
        grad = (gate[own] * differ * valid_col / jnp.sqrt(valid_total)).astype(jnp.bfloat16)
        outs.append(out)
        all_grads.append(spread_out(grad, c))

    grad_act = summed(all_grads, lambda t, c: down[:, at(t, c)], across)
    unused, pullback = jax.vjp(gelu_tanh, hidden_pre)
    grad_pre = pullback(grad_act)[0].astype(jnp.bfloat16)

    def over_all_tokens(found, right):
        return jnp.concatenate(
            [over_tokens(jnp.concatenate(found[c][t], axis=0), right).astype(jnp.bfloat16) for t, c in parts], axis=0
        )

    down_found = over_all_tokens(all_grads, hidden_act)
    if cores > 2:
        own_normed, grad_pre = lax.optimization_barrier((normed, grad_pre))
        all_normed = [spread_out(own_normed[:, c * part : (c + 1) * part], c) for c in range(pieces)]
    up_found = over_all_tokens(all_normed, grad_pre)
    taken = block // sides
    arrivals = []
    for k in range(count):
        arrivals.append([])
        for to in range(sides):
            start = feature_offsets[k] + to * taken
            piece = jnp.concatenate(
                [lax.dynamic_slice_in_dim(found, start, taken, 0) for found in (up_found, down_found)], axis=0
            )
            arrivals[k].append(sent(k, piece, to))
    up_share, down_share = received(side, [peer * share for peer in peers], arrivals, hidden)
    return (jnp.concatenate(outs, axis=1)[None], up_share, down_share.T)


def solution(mesh):
    placed = (
        P("dp", "mp"),
        P("side", "dp", "mp"),
        P("side", "mp", "dp"),
        P("side", None, None, None),
        P("dp"),
        P(),
    )
    return jax.shard_map(
        shards,
        mesh=mesh,
        in_specs=placed,
        out_specs=(P("side", "dp", "mp"), P(("dp", "side"), "mp"), P("mp", ("dp", "side"))),
        check_vma=False,
    )
```

```python
import jax
import jax.numpy as jnp
from jax import lax
from jax.experimental import pallas as pl
from jax.experimental.pallas import tpu as pltpu
from jax.sharding import PartitionSpec as P

LANES = 128
TILE_ROWS = 16
DIGIT = 256


NO_COST = pl.CostEstimate(flops=0, bytes_accessed=0, transcendentals=0)


def gelu_tanh(values):
    return jax.nn.gelu(values, approximate=True)


def product(left, right):
    return jnp.dot(left, right, preferred_element_type=jnp.float32)


def over_tokens(left, right):
    return lax.dot_general(left, right, (((0,), (0,)), ((), ())), preferred_element_type=jnp.float32)


def across(left, right):
    return lax.dot_general(left, right, (((1,), (1,)), ((), ())), preferred_element_type=jnp.float32)


def ring_order(count):
    return list(range(0, count, 2)) + list(range(1, count, 2))[::-1]


def ring_shift(x, by):
    order = ring_order(lax.axis_size("dp"))
    count = len(order)
    return lax.ppermute(x, "dp", [(order[p], order[(p + by) % count]) for p in range(count)])


def from_core(x, by):
    count = lax.axis_size("mp")
    return lax.ppermute(x, "mp", [((c + by) % count, c) for c in range(count)])


def ring_gather(x, sign):
    count = lax.axis_size("dp")
    found = [x] * count
    there = back = x
    for hop in range(1, count // 2 + 1):
        there = ring_shift(there, sign)
        found[(-sign * hop) % count] = there
        if hop <= (count - 1) // 2:
            back = ring_shift(back, -sign)
            found[(sign * hop) % count] = back
    return found


def ring_scatter(terms, sign):
    count = lax.axis_size("dp")
    total = terms[0]
    for way, hops in ((sign, count // 2), (-sign, (count - 1) // 2)):
        if hops:
            running = terms[(way * hops) % count]
            for hop in range(hops - 1, -1, -1):
                arrived = ring_shift(running.astype(jnp.bfloat16), way).astype(jnp.float32)
                if hop:
                    running = arrived + terms[(way * hop) % count]
                else:
                    total = total + arrived
    return total


def in_vmem(count):
    return [pl.BlockSpec(memory_space=pltpu.VMEM)] * count


def placed_along(axis, offsets, pieces, length):
    shape = list(pieces[0].shape)
    shape[axis] = length
    result = jnp.zeros(shape, pieces[0].dtype)
    for k, piece in enumerate(pieces):
        result = lax.dynamic_update_slice_in_dim(result, piece, offsets[k], axis)
    return result


def placed(axis, scalars, arrays, pieces, shape):
    count = len(pieces)

    def kernel(scalar_ref, *refs):
        *taken, result, semaphores = refs
        copies = []
        for k, piece in enumerate(pieces):
            source = piece(taken, scalar_ref)
            extent = source.shape[axis]
            where = pl.ds(pl.multiple_of(scalar_ref[k], extent), extent)
            target = result.at[where, :] if axis == 0 else result.at[:, where]
            copies.append(pltpu.make_async_copy(source, target, semaphores.at[k]))
            copies[-1].start()
        for copy in copies:
            copy.wait()

    return pl.pallas_call(
        kernel,
        out_shape=jax.ShapeDtypeStruct(shape, arrays[0].dtype),
        in_specs=[pl.BlockSpec(memory_space=pltpu.SMEM)] + [pl.BlockSpec(memory_space=pl.ANY)] * len(arrays),
        out_specs=pl.BlockSpec(memory_space=pltpu.VMEM),
        scratch_shapes=[pltpu.SemaphoreType.DMA((count,))],
        compiler_params=pltpu.CompilerParams(vmem_limit_bytes=16 << 20),
        cost_estimate=NO_COST,
        name="placed",
    )(jnp.stack(scalars).astype(jnp.int32), *arrays)


def stacked(pieces):
    rows, columns = pieces[0].shape
    if columns % LANES:
        return jnp.concatenate(pieces, axis=0)

    def kernel(*refs):
        for k, ref in enumerate(refs[:-1]):
            refs[-1][k * rows : k * rows + rows, :] = ref[...]

    return pl.pallas_call(
        kernel,
        out_shape=jax.ShapeDtypeStruct((rows * len(pieces), columns), pieces[0].dtype),
        in_specs=in_vmem(len(pieces)),
        out_specs=pl.BlockSpec(memory_space=pltpu.VMEM),
        compiler_params=pltpu.CompilerParams(vmem_limit_bytes=16 << 20),
        cost_estimate=NO_COST,
        name="stacked",
    )(*pieces)


def stacked_parts(parts):
    rows, columns = parts[0][0].shape
    count = len(parts[0])
    flat = [piece for pieces in parts for piece in pieces]

    def kernel(*refs):
        for k, ref in enumerate(refs[:-1]):
            at = k % count * rows
            refs[-1][k // count, at : at + rows, :] = ref[...]

    return pl.pallas_call(
        kernel,
        out_shape=jax.ShapeDtypeStruct((len(parts), rows * count, columns), parts[0][0].dtype),
        in_specs=in_vmem(len(flat)),
        out_specs=pl.BlockSpec(memory_space=pltpu.VMEM),
        compiler_params=pltpu.CompilerParams(vmem_limit_bytes=24 << 20),
        cost_estimate=NO_COST,
        name="stacked_parts",
    )(*flat)


def modulated_up(tokens, rows, timesteps, places, table, up):
    _, kinds, features = table.shape
    images = timesteps.shape[0]
    _, sent_rows, part = tokens[0].shape
    total_rows = images * rows
    units = up.shape[1]
    halves = len(tokens) // 2

    def kernel(step_ref, place_ref, table_ref, up_ref, *refs):
        taken, (own_out, other_out, pre_ref, act_ref) = refs[: 2 * halves], refs[2 * halves :]
        total = sum(jnp.sum(ref[0, :rows].astype(jnp.float32), axis=-1, keepdims=True) for ref in taken)
        average = total / features
        squares = sum(
            jnp.sum((ref[0, :rows].astype(jnp.float32) - average) ** 2, axis=-1, keepdims=True) for ref in taken
        )
        inverse = lax.rsqrt(squares / features + 1e-06)
        pre = jnp.zeros((rows, units), jnp.float32)
        for place, ref in enumerate(taken):
            where = slice(place * part, (place + 1) * part)
            scaled = (ref[0, :rows].astype(jnp.float32) - average) * inverse
            here = pl.ds(pl.multiple_of(place_ref[place], LANES), part)
            value = scaled * (1.0 + table_ref[0, 1:2, here]) + table_ref[0, 0:1, here]
            value = value.astype(jnp.bfloat16)
            (own_out, other_out)[place // halves][place % halves] = value
            pre = pre + jnp.dot(value, up_ref[where, :], preferred_element_type=jnp.float32)
        pre_ref[...] = pre
        act_ref[...] = gelu_tanh(pre).astype(jnp.bfloat16)

    rows_of = pl.BlockSpec((halves, rows, part), lambda i, step_ref, place_ref: (0, i, 0))
    units_of = pl.BlockSpec((rows, units), lambda i, step_ref, place_ref: (i, 0))
    return pl.pallas_call(
        kernel,
        grid_spec=pltpu.PrefetchScalarGridSpec(
            num_scalar_prefetch=2,
            grid=(images,),
            in_specs=[
                pl.BlockSpec((1, kinds, features), lambda i, step_ref, place_ref: (step_ref[i], 0, 0)),
                pl.BlockSpec((features, units), lambda i, step_ref, place_ref: (0, 0)),
            ]
            + [pl.BlockSpec((1, sent_rows, part), lambda i, step_ref, place_ref: (i, 0, 0))] * len(tokens),
            out_specs=[rows_of, rows_of, units_of, units_of],
        ),
        out_shape=[jax.ShapeDtypeStruct((halves, total_rows, part), jnp.bfloat16)] * 2
        + [jax.ShapeDtypeStruct((total_rows, units), kind) for kind in (jnp.float32, jnp.bfloat16)],
        compiler_params=pltpu.CompilerParams(vmem_limit_bytes=40 << 20),
        cost_estimate=NO_COST,
        name="modulated_up",
    )(timesteps, places, table, up, *tokens)


def act_gradient(own, other, down, pre, rows):
    halves, total_rows, part = own.shape
    units, features = down.shape

    def kernel(down_ref, pre_ref, own_ref, other_ref, out_ref):
        total = jnp.zeros((rows, units), jnp.float32)
        for place in range(2 * halves):
            ref = (own_ref, other_ref)[place // halves]
            total = total + across(ref[place % halves], down_ref[:, place * part : (place + 1) * part])
        unused, pullback = jax.vjp(gelu_tanh, pre_ref[...])
        out_ref[...] = pullback(total)[0].astype(jnp.bfloat16)

    rows_of = pl.BlockSpec((halves, rows, part), lambda i: (0, i, 0))
    return pl.pallas_call(
        kernel,
        grid=(total_rows // rows,),
        in_specs=[
            pl.BlockSpec((units, features), lambda i: (0, 0)),
            pl.BlockSpec((rows, units), lambda i: (i, 0)),
            rows_of,
            rows_of,
        ],
        out_specs=pl.BlockSpec((rows, units), lambda i: (i, 0)),
        out_shape=jax.ShapeDtypeStruct((total_rows, units), jnp.bfloat16),
        compiler_params=pltpu.CompilerParams(vmem_limit_bytes=32 << 20),
        cost_estimate=NO_COST,
        name="act_gradient",
    )(down, pre, own, other)


def weight_gradient(lefts, rights, steps, block, one_side):
    halves, _, part = lefts[0][0].shape
    units = rights[0].shape[1]
    each = part // block
    count = halves * each
    half = block // 2
    groups = len(lefts)
    skipped = half // LANES * LANES

    def kernel(step_ref, *refs):
        left_refs, right_refs, outs = refs[: 2 * groups], refs[2 * groups : 3 * groups], refs[3 * groups :]

        def found(which, begin, end):
            return sum(
                over_tokens(left_refs[2 * g + which][0, :, begin:end], right_refs[g][...]) for g in range(groups)
            ).astype(jnp.bfloat16)

        for which in range(2):
            step = step_ref[which * count + pl.program_id(0)]
            if not one_side:
                value = found(which, 0, block)
                outs[0][step] = value[:half]
                outs[1][step] = value[half:]
                continue

            @pl.when(step_ref[2 * count] == 0)
            def _():
                outs[0][step] = found(which, 0, block - skipped)[:half]

            @pl.when(step_ref[2 * count] == 1)
            def _():
                outs[0][step] = found(which, skipped, block)[half - skipped :]

    left_specs = [
        pl.BlockSpec((1, x.shape[1], block), lambda i, step_ref: (i // each, 0, i % each)) for pair in lefts for x in pair
    ]
    right_specs = [pl.BlockSpec(x.shape, lambda i, step_ref: (0, 0)) for x in rights]
    results = 1 if one_side else 2
    return pl.pallas_call(
        kernel,
        grid_spec=pltpu.PrefetchScalarGridSpec(
            num_scalar_prefetch=1,
            grid=(count,),
            in_specs=left_specs + right_specs,
            out_specs=[pl.BlockSpec((2 * count, half, units), lambda i, step_ref: (0, 0, 0))] * results,
        ),
        out_shape=[jax.ShapeDtypeStruct((2 * count, half, units), jnp.bfloat16)] * results,
        compiler_params=pltpu.CompilerParams(vmem_limit_bytes=40 << 20),
        cost_estimate=NO_COST,
        name="weight_gradient",
    )(steps, *[x for pair in lefts for x in pair], *rights)


def after(x, *others):
    return lax.optimization_barrier((x, others))[0]


def received(offsets, arrivals, width):
    rows, share = arrivals[0].shape
    if share % LANES:
        result = jnp.zeros((rows, width), jnp.float32)
        for k, piece in enumerate(arrivals):
            result = lax.dynamic_update_slice_in_dim(result, piece.astype(jnp.float32), offsets[k], 1)
        return result

    def kernel(offset_ref, *refs):
        for k, ref in enumerate(refs[:-1]):
            where = pl.ds(pl.multiple_of(offset_ref[k], share), share)
            refs[-1][:, where] = ref[...].astype(jnp.float32)

    return pl.pallas_call(
        kernel,
        out_shape=jax.ShapeDtypeStruct((rows, width), jnp.float32),
        in_specs=[pl.BlockSpec(memory_space=pltpu.SMEM)] + in_vmem(len(arrivals)),
        out_specs=pl.BlockSpec(memory_space=pltpu.VMEM),
        compiler_params=pltpu.CompilerParams(vmem_limit_bytes=16 << 20),
        cost_estimate=NO_COST,
        name="received",
    )(jnp.stack(offsets).astype(jnp.int32), *arrivals)


def partner(index, step, count):
    return index ^ step if count & (count - 1) == 0 else (step - index) % count


def shards(tokens, up_weight, down_weight, mod_table, timesteps, valid_counts):
    count, cores, sides = lax.axis_size("dp"), lax.axis_size("mp"), lax.axis_size("side")
    me, core, side = lax.axis_index("dp"), lax.axis_index("mp"), lax.axis_index("side")
    is_student = side == 1
    rows, width = tokens.shape
    pieces = 2 if width % (2 * LANES) == 0 and cores == 2 else 1
    part = width // pieces
    block, hidden = up_weight.shape[1:]
    share = hidden // count
    features = block * count
    first = core * width if cores == 2 else 0
    peers = [partner(me, step, count) for step in range(count)]
    feature_offsets = [(peer * block - first) % features for peer in peers]

    def sent(step, piece):
        pairs = [(i, partner(i, step, count)) for i in range(count)]
        return piece if all(i == j for i, j in pairs) else lax.ppermute(piece, "dp", pairs)

    wide = tokens.astype(jnp.float32)
    own_mean = jnp.mean(wide, axis=-1, keepdims=True)
    own_spread = jnp.sum((wide - own_mean) ** 2, axis=-1, keepdims=True)
    moments = jnp.concatenate([own_mean, own_spread], axis=1)
    if cores == 2:
        all_moments = jnp.stack([moments, from_core(moments, 1)])
    else:
        all_moments = lax.all_gather(moments, "mp")
    average = jnp.mean(all_moments[:, :, :1], axis=0)
    spread = jnp.sum(all_moments[:, :, 1:] + width * (all_moments[:, :, :1] - average) ** 2, axis=0)
    scaled = (wide - average) * lax.rsqrt(spread / features + 1e-06)
    modulation = lax.dynamic_slice(
        mod_table[0], (timesteps[0], 0, core * width), (1, mod_table.shape[2], width)
    )[0]
    normed = (scaled * (1.0 + modulation[1]) + modulation[0]).astype(jnp.bfloat16)
    gate = modulation[2]

    def own_features(array):
        return [ring_gather(array[:, c * part : (c + 1) * part], 1 if c % 2 == 0 else -1) for c in range(pieces)]

    def widened(found):
        own = stacked(found)
        if cores == 2:
            return [own, from_core(own, 1)]
        everything = lax.all_gather(own, "mp")
        return [everything[t] for t in range(cores)]

    def at(t, c):
        start = t * width + c * part
        return slice(start, start + part)

    parts = [(t, c) for t in range(cores) for c in range(pieces)]

    normed_found = own_features(normed)
    ups = [sent(k, lax.dynamic_slice_in_dim(up_weight[0], peers[k] * share, share, 1)) for k in range(count)]
    downs = []
    for k in range(count):
        piece = lax.dynamic_slice_in_dim(down_weight[0], peers[k] * share, share, 0)
        hop = min((k + 1) // 2, (count - 1) // 2)
        if k and hop:
            piece = after(piece, *[found[way] for found in normed_found for way in (hop, count - hop)])
        downs.append(sent(k, piece))
    up = placed_along(0, feature_offsets, ups, features)
    down = placed_along(1, feature_offsets, downs, features)

    all_normed = [widened(found) for found in normed_found]
    hidden_pre = sum(product(all_normed[c][t], up[at(t, c)]) for t, c in parts)
    hidden_act = gelu_tanh(hidden_pre).astype(jnp.bfloat16)

    valid_col = (jnp.arange(rows, dtype=jnp.int32) < valid_counts[me]).astype(jnp.float32)[:, None]
    valid_total = jnp.sum(valid_counts).astype(jnp.float32)

    def of_student(x):
        return jnp.where(is_student, x, lax.ppermute(x, "side", [(1, 0)]))

    student_gate = of_student(gate)
    student_act = of_student(hidden_act)

    outs, grads = [], []
    for c in range(pieces):
        if cores == 2:
            away = product(hidden_act, down[:, at(1, c)]).astype(jnp.bfloat16)
            term = product(hidden_act, down[:, at(0, c)]) + from_core(away, 1).astype(jnp.float32)
        else:
            term = lax.psum_scatter(
                product(hidden_act, down).astype(jnp.bfloat16), "mp", scatter_dimension=1, tiled=True
            ).astype(jnp.float32)
        mixed = ring_scatter([term[r * rows : (r + 1) * rows] for r in range(count)], 1 if c % 2 == 0 else -1)
        own = slice(c * part, (c + 1) * part)
        out = (wide[:, own] + gate[own] * mixed).astype(jnp.bfloat16)
        other = lax.ppermute(out, "side", [(0, 1), (1, 0)])
        differ = out.astype(jnp.float32) - other.astype(jnp.float32)
        differ = jnp.where(is_student, differ, -differ)
        grad = (student_gate[own] * differ * valid_col / jnp.sqrt(valid_total)).astype(jnp.bfloat16)
        outs.append(out)
        grads.append(grad)

    grads_found = lax.optimization_barrier(own_features(jnp.concatenate(grads, axis=1)))
    all_grads = [widened(found) for found in grads_found]

    def over_all_tokens(found, right):
        return jnp.concatenate([over_tokens(found[c][t], right).astype(jnp.bfloat16) for t, c in parts], axis=0)

    taken = block // sides

    def delivered(own):
        own = own.reshape(count * taken, share)
        arrivals = [
            sent(k, lax.dynamic_slice_in_dim(own, feature_offsets[k] // sides, taken, 0)) for k in range(count)
        ]
        return received([peer * share for peer in peers], arrivals, hidden)

    down_found = over_all_tokens(all_grads, student_act).reshape(count, sides, taken, share)
    down_share = delivered(lax.dynamic_index_in_dim(down_found, side, 1, keepdims=False))
    grad_act = sum(across(all_grads[c][t], down[:, at(t, c)]) for t, c in parts)
    unused, pullback = jax.vjp(gelu_tanh, hidden_pre)
    grad_pre = pullback(grad_act)[0].astype(jnp.bfloat16)
    if cores > 2:
        own_normed, grad_pre = lax.optimization_barrier((normed, grad_pre))
        all_normed = [widened(found) for found in own_features(own_normed)]
    up_found = over_all_tokens(all_normed, grad_pre).reshape(count, sides, taken, share)
    up_share = delivered(jnp.where(is_student, up_found[:, 1], lax.ppermute(up_found[:, 0], "side", [(1, 0)])))
    return (jnp.concatenate(outs, axis=1)[None], up_share, down_share.T)


def paired_shards(tokens, up_weight, down_weight, mod_table, timesteps, valid_counts):
    count = lax.axis_size("dp")
    me, core, side = lax.axis_index("dp"), lax.axis_index("mp"), lax.axis_index("side")
    is_student = side == 1
    rows, width = tokens.shape
    part = width // 2
    block, hidden = up_weight.shape[1:]
    share = hidden // count
    features = block * count
    taken = block // 2
    peers = [partner(me, step, count) for step in range(count)]
    swap = [(0, 1), (1, 0)]

    def feature_offset(owner):
        start = owner * block
        t, c = (start // width + core) % 2, (start // part % 2 + side) % 2
        return (2 * t + c) * part + start % part

    feature_offsets = [feature_offset(peer) for peer in peers]

    def sent(step, piece):
        pairs = [(i, partner(i, step, count)) for i in range(count)]
        return piece if all(i == j for i, j in pairs) else lax.ppermute(piece, "dp", pairs)

    def halves(array):
        return [lax.dynamic_slice_in_dim(array, ((side + c) % 2) * part, part, array.ndim - 1) for c in range(2)]

    def of_student(x):
        return jnp.where(is_student, x, lax.ppermute(x, "side", [(1, 0)]))

    part_places = jnp.stack([(core + t) % 2 * width + (side + c) % 2 * part for t in range(2) for c in range(2)])
    part_places = part_places.astype(jnp.int32)
    gate = lax.dynamic_slice(mod_table[0], (timesteps[0], 2, core * width), (1, 1, width)).reshape(width)
    gates = halves(gate)
    student_gate = of_student(gate)

    farthest = count // 2
    near_images = [r for r in range(count) if min(r, count - r) <= farthest - 2]
    far_images = [farthest, farthest - 1, farthest + 1]
    steps = jnp.zeros((count,), jnp.int32).at[jnp.stack(feature_offsets) // block].set(jnp.arange(count, dtype=jnp.int32))
    steps = jnp.concatenate([steps, side[None].astype(jnp.int32)])

    token_halves = halves(tokens)
    column = lax.broadcasted_iota(jnp.int32, (TILE_ROWS, part), 1)
    digits = jnp.where(column == 0, timesteps[0] % DIGIT, jnp.where(column == 1, timesteps[0] // DIGIT, 0))
    there = back = jnp.concatenate([token_halves[0], digits.astype(jnp.bfloat16)], axis=0)
    round_ring = [there] + [None] * (count - 1)
    far, near = list(range(count - 1, farthest - 1, -1)), list(range(farthest - 1, 0, -1))
    arrived = []
    for hop in range(1, farthest + 1):
        there = ring_shift(there, 1)
        round_ring[-hop % count] = there
        if hop <= (count - 1) // 2:
            back = ring_shift(back, -1)
            round_ring[hop] = back
        arrived.append([there, back])

    columns, column, row = count // 2, me // 2, me % 2

    def over_columns(step, piece):
        pairs = [(i, 2 * partner(i // 2, step, columns) + i % 2) for i in range(count)]
        return lax.ppermute(piece, "dp", pairs) if step else piece

    def over_rows(piece):
        return lax.ppermute(piece, "dp", [(i, i ^ 1) for i in range(count)])

    column_peers = [partner(column, step, columns) for step in range(columns)]
    steps_out = list(range(columns - 1, -1, -1))
    up_pairs = [None] * columns
    for step in steps_out:
        piece = lax.dynamic_slice_in_dim(up_weight[0], column_peers[step] * 2 * share, 2 * share, 1)
        up_pairs[step] = over_columns(step, piece)
    up_passed = over_rows(jnp.stack([lax.dynamic_slice_in_dim(x, (1 - row) * share, share, 1) for x in up_pairs]))
    by_row = down_weight[0].reshape(columns, 2, share, block)
    down_kept = lax.dynamic_index_in_dim(by_row, row, 1, keepdims=False)
    down_passed = over_rows(lax.dynamic_index_in_dim(by_row, 1 - row, 1, keepdims=False))
    down_pairs = [None] * columns
    for step in steps_out:
        piece = jnp.stack(
            [lax.dynamic_index_in_dim(x, column_peers[step], 0, keepdims=False) for x in (down_kept, down_passed)]
        )
        down_pairs[step] = over_columns(step, after(piece, *up_pairs[1:]))

    def up_piece(k):
        if k % 2:
            return lambda refs, scalar_ref: refs[columns].at[k // 2]
        return lambda refs, scalar_ref: refs[k // 2].at[
            :, pl.ds(pl.multiple_of(scalar_ref[count] * share, share), share)
        ]

    def down_piece(k):
        return lambda refs, scalar_ref: refs[k // 2].at[k % 2]

    def all_features(images):
        first = stacked([round_ring[r] for r in images])
        crossed = after(lax.ppermute(first, "side", swap), *up_pairs[1:])
        pair = [first, crossed]
        steps_taken = first.reshape(len(images), rows + TILE_ROWS, part)[:, rows, :2].astype(jnp.int32)
        shaped = [x.reshape(len(images), rows + TILE_ROWS, part) for x in pair + [from_core(x, 1) for x in pair]]
        return shaped, steps_taken[:, 0] + DIGIT * steps_taken[:, 1]

    near_tokens, near_steps = all_features(near_images)
    far_tokens, far_steps = all_features(far_images)
    scalars = feature_offsets + [row]
    up = placed(0, scalars, up_pairs + [up_passed], [up_piece(k) for k in range(count)], (features, share))
    table = mod_table[0]
    *far_normed, far_pre, far_act = modulated_up(far_tokens, rows, far_steps, part_places, table, up)
    near_tokens = after(near_tokens, far_act)
    *near_normed, near_pre, near_act = modulated_up(near_tokens, rows, near_steps, part_places, table, up)
    down_pairs = after(down_pairs, near_act)
    down = placed(1, scalars, down_pairs, [down_piece(k) for k in range(count)], (share, features))

    student_acts = [of_student(near_act), of_student(far_act)]
    valid_col = (jnp.arange(rows, dtype=jnp.int32) < valid_counts[me]).astype(jnp.float32)[:, None]
    valid_total = jnp.sum(valid_counts).astype(jnp.float32)
    terms = [[None] * count, [None] * count]
    earlier = []
    groups = [(far_images[:1], far_act[:rows]), (far_images[1:], far_act[rows:]), (near_images, near_act)]
    earlier = []
    for images, act in groups:
        act = after(act, *earlier)
        from_other = from_core(product(act, down[:, width:]).astype(jnp.bfloat16), 1)
        earlier = [from_other]
        for c in range(2):
            here = slice(c * part, (c + 1) * part)
            term = product(act, down[:, here]) + from_other[:, here].astype(jnp.float32)
            for k, r in enumerate(images):
                terms[c][r] = term[k * rows : (k + 1) * rows]
    mixed = [ring_scatter(terms[c], 1 if c == 0 else -1) for c in range(2)]
    mixed, student_acts, student_gate = lax.optimization_barrier((mixed, student_acts, student_gate))
    student_gates = halves(student_gate)
    outs = [(token_halves[c].astype(jnp.float32) + gates[c] * mixed[c]).astype(jnp.bfloat16) for c in range(2)]
    found = []
    for c in range(2):
        differ = outs[c].astype(jnp.float32) - lax.ppermute(outs[1 - c], "side", swap).astype(jnp.float32)
        differ = jnp.where(is_student, differ, -differ)
        grad = (student_gates[c] * differ * valid_col / jnp.sqrt(valid_total)).astype(jnp.bfloat16)
        found.append([grad] + [None] * (count - 1))

    there, back = [found[c][0] for c in range(2)], [found[c][0] for c in range(2)]
    for hop in range(1, farthest + 1):
        if hop == farthest:
            near_own = stacked_parts([[found[c][r] for r in near_images] for c in range(2)])
            near_grads = [near_own, from_core(near_own, 1)]
            there = after(there, *near_grads)
        for c, way in ((0, 1), (1, -1)):
            there[c] = ring_shift(there[c], way)
            found[c][(-way * hop) % count] = there[c]
            if hop <= (count - 1) // 2:
                back[c] = ring_shift(back[c], -way)
                found[c][(way * hop) % count] = back[c]
    near_grad_pre = act_gradient(*near_grads, down, near_pre, rows)
    far_found = [[found[c][r] for r in far_images] for c in range(2)]
    far_own = stacked_parts(after(far_found, *there, near_grad_pre))
    far_grads = [far_own, from_core(far_own, 1)]

    (down_found,) = weight_gradient([near_grads, far_grads], student_acts, steps, block, True)
    down_arrived = [sent(k, down_found[k]) for k in range(count)]
    far_grad_pre = act_gradient(*after(far_grads, down_found), down, far_pre, rows)
    far_grad_pre = after(far_grad_pre, down_arrived[far[0]])
    up_found = weight_gradient([near_normed, far_normed], [near_grad_pre, far_grad_pre], steps, block, False)
    handed = after(up_found[0], down_arrived[far[2]])
    split = count // 2
    handed = [lax.ppermute(x, "side", [(1, 0)]) for x in (handed[split:], handed[:split])]
    first = jnp.where(is_student, up_found[1][split:], after(handed[0], *[down_arrived[k] for k in near]))
    up_arrived = [None] * split + [sent(k, first[k - split]) for k in range(split, count)]
    second = jnp.where(is_student, up_found[1][:split], after(handed[1], up_arrived[far[0]]))
    up_arrived[:split] = [sent(k, second[k]) for k in range(split)]
    places = [peer * share for peer in peers]
    out = jnp.concatenate(
        [jnp.where(side == 0, outs[0], outs[1]), jnp.where(side == 0, outs[1], outs[0])], axis=1
    )
    return (out[None], received(places, up_arrived, hidden), received(places, down_arrived, hidden).T)


def solution(mesh):
    placed = (
        P("dp", "mp"),
        P("side", "dp", "mp"),
        P("side", "mp", "dp"),
        P("side", None, None, None),
        P("dp"),
        P(),
    )
    paired = mesh.shape["mp"] == mesh.shape["side"] == 2 and mesh.shape["dp"] in (8, 16, 32)
    return jax.shard_map(
        paired_shards if paired else shards,
        mesh=mesh,
        in_specs=placed,
        out_specs=(P("side", "dp", "mp"), P(("dp", "side"), "mp"), P("mp", ("dp", "side"))),
        check_vma=False,
    )
```

```python
import jax
import jax.numpy as jnp
from jax import lax
from jax.experimental import pallas as pl
from jax.experimental.pallas import tpu as pltpu
from jax.sharding import PartitionSpec as P

LANES = 128
TILE_ROWS = 16
DIGIT = 256


NO_COST = pl.CostEstimate(flops=1, bytes_accessed=1, transcendentals=0)


def gelu_tanh(values):
    return jax.nn.gelu(values, approximate=True)


def product(left, right):
    return jnp.dot(left, right, preferred_element_type=jnp.float32)


def over_tokens(left, right):
    return lax.dot_general(left, right, (((0,), (0,)), ((), ())), preferred_element_type=jnp.float32)


def across(left, right):
    return lax.dot_general(left, right, (((1,), (1,)), ((), ())), preferred_element_type=jnp.float32)


def ring_order(count):
    return list(range(0, count, 2)) + list(range(1, count, 2))[::-1]


def ring_shift(x, by):
    order = ring_order(lax.axis_size("dp"))
    count = len(order)
    return lax.ppermute(x, "dp", [(order[p], order[(p + by) % count]) for p in range(count)])


def from_core(x, by):
    count = lax.axis_size("mp")
    return lax.ppermute(x, "mp", [((c + by) % count, c) for c in range(count)])


def ring_gather(x, sign):
    count = lax.axis_size("dp")
    found = [x] * count
    there = back = x
    for hop in range(1, count // 2 + 1):
        there = ring_shift(there, sign)
        found[(-sign * hop) % count] = there
        if hop <= (count - 1) // 2:
            back = ring_shift(back, -sign)
            found[(sign * hop) % count] = back
    return found


def ring_scatter(terms, sign):
    count = lax.axis_size("dp")
    total = terms[0]
    for way, hops in ((sign, count // 2), (-sign, (count - 1) // 2)):
        if hops:
            running = terms[(way * hops) % count]
            for hop in range(hops - 1, -1, -1):
                arrived = ring_shift(running.astype(jnp.bfloat16), way).astype(jnp.float32)
                if hop:
                    running = arrived + terms[(way * hop) % count]
                else:
                    total = total + arrived
    return total


def in_vmem(count):
    return [pl.BlockSpec(memory_space=pltpu.VMEM)] * count


def placed_along(axis, offsets, pieces, length):
    shape = list(pieces[0].shape)
    shape[axis] = length
    result = jnp.zeros(shape, pieces[0].dtype)
    for k, piece in enumerate(pieces):
        result = lax.dynamic_update_slice_in_dim(result, piece, offsets[k], axis)
    return result


def placed(axis, scalars, arrays, pieces, shape):
    count = len(pieces)

    def kernel(scalar_ref, *refs):
        *taken, result, semaphores = refs
        copies = []
        for k, piece in enumerate(pieces):
            source = piece(taken, scalar_ref)
            extent = source.shape[axis]
            where = pl.ds(pl.multiple_of(scalar_ref[k], extent), extent)
            target = result.at[where, :] if axis == 0 else result.at[:, where]
            copies.append(pltpu.make_async_copy(source, target, semaphores.at[k]))
            copies[-1].start()
        for copy in copies:
            copy.wait()

    return pl.pallas_call(
        kernel,
        out_shape=jax.ShapeDtypeStruct(shape, arrays[0].dtype),
        in_specs=[pl.BlockSpec(memory_space=pltpu.SMEM)] + [pl.BlockSpec(memory_space=pl.ANY)] * len(arrays),
        out_specs=pl.BlockSpec(memory_space=pltpu.VMEM),
        scratch_shapes=[pltpu.SemaphoreType.DMA((count,))],
        compiler_params=pltpu.CompilerParams(vmem_limit_bytes=16 << 20),
        cost_estimate=NO_COST,
        name="placed",
    )(jnp.stack(scalars).astype(jnp.int32), *arrays)


def by_columns(x, count):
    rows, columns = x.shape
    columns //= count

    def kernel(x_ref, result_ref):
        for k in range(count):
            result_ref[k * rows : (k + 1) * rows, :] = x_ref[:, k * columns : (k + 1) * columns]

    return pl.pallas_call(
        kernel,
        out_shape=jax.ShapeDtypeStruct((rows * count, columns), x.dtype),
        in_specs=in_vmem(1),
        out_specs=pl.BlockSpec(memory_space=pltpu.VMEM),
        compiler_params=pltpu.CompilerParams(vmem_limit_bytes=16 << 20),
        cost_estimate=NO_COST,
        name="by_columns",
    )(x)


def stacked(pieces):
    columns = pieces[0].shape[1]
    starts = [sum(piece.shape[0] for piece in pieces[:k]) for k in range(len(pieces) + 1)]
    if columns % LANES:
        return jnp.concatenate(pieces, axis=0)

    def kernel(*refs):
        for k, ref in enumerate(refs[:-1]):
            refs[-1][starts[k] : starts[k + 1], :] = ref[...]

    return pl.pallas_call(
        kernel,
        out_shape=jax.ShapeDtypeStruct((starts[-1], columns), pieces[0].dtype),
        in_specs=in_vmem(len(pieces)),
        out_specs=pl.BlockSpec(memory_space=pltpu.VMEM),
        compiler_params=pltpu.CompilerParams(vmem_limit_bytes=16 << 20),
        cost_estimate=NO_COST,
        name="stacked",
    )(*pieces)


def stacked_parts(parts):
    rows, columns = parts[0][0].shape
    count = len(parts[0])
    flat = [piece for pieces in parts for piece in pieces]

    def kernel(*refs):
        for k, ref in enumerate(refs[:-1]):
            at = k % count * rows
            refs[-1][k // count, at : at + rows, :] = ref[...]

    return pl.pallas_call(
        kernel,
        out_shape=jax.ShapeDtypeStruct((len(parts), rows * count, columns), parts[0][0].dtype),
        in_specs=in_vmem(len(flat)),
        out_specs=pl.BlockSpec(memory_space=pltpu.VMEM),
        compiler_params=pltpu.CompilerParams(vmem_limit_bytes=24 << 20),
        cost_estimate=NO_COST,
        name="stacked_parts",
    )(*flat)


def modulated_up(tokens, rows, timesteps, places, table, up):
    _, kinds, features = table.shape
    images = timesteps.shape[0]
    _, sent_rows, part = tokens[0].shape
    total_rows = images * rows
    units = up.shape[1]
    halves = len(tokens) // 2

    def kernel(step_ref, place_ref, table_ref, up_ref, *refs):
        taken, (own_out, other_out, pre_ref, act_ref) = refs[: 2 * halves], refs[2 * halves :]
        total = sum(jnp.sum(ref[0, :rows].astype(jnp.float32), axis=-1, keepdims=True) for ref in taken)
        average = total / features
        squares = sum(
            jnp.sum((ref[0, :rows].astype(jnp.float32) - average) ** 2, axis=-1, keepdims=True) for ref in taken
        )
        inverse = lax.rsqrt(squares / features + 1e-06)
        pre = jnp.zeros((rows, units), jnp.float32)
        for place, ref in enumerate(taken):
            scaled = (ref[0, :rows].astype(jnp.float32) - average) * inverse
            here = pl.ds(pl.multiple_of(place_ref[place], LANES), part)
            value = scaled * (1.0 + table_ref[0, 1:2, here]) + table_ref[0, 0:1, here]
            value = value.astype(jnp.bfloat16)
            (own_out, other_out)[place // halves][place % halves] = value
            pre = pre + jnp.dot(value, up_ref[here, :], preferred_element_type=jnp.float32)
        pre_ref[...] = pre
        act_ref[...] = gelu_tanh(pre).astype(jnp.bfloat16)

    rows_of = pl.BlockSpec((halves, rows, part), lambda i, step_ref, place_ref: (0, i, 0))
    units_of = pl.BlockSpec((rows, units), lambda i, step_ref, place_ref: (i, 0))
    return pl.pallas_call(
        kernel,
        grid_spec=pltpu.PrefetchScalarGridSpec(
            num_scalar_prefetch=2,
            grid=(images,),
            in_specs=[
                pl.BlockSpec((1, kinds, features), lambda i, step_ref, place_ref: (step_ref[i], 0, 0)),
                pl.BlockSpec((features, units), lambda i, step_ref, place_ref: (0, 0)),
            ]
            + [pl.BlockSpec((1, sent_rows, part), lambda i, step_ref, place_ref: (i, 0, 0))] * len(tokens),
            out_specs=[rows_of, rows_of, units_of, units_of],
        ),
        out_shape=[jax.ShapeDtypeStruct((halves, total_rows, part), jnp.bfloat16)] * 2
        + [jax.ShapeDtypeStruct((total_rows, units), kind) for kind in (jnp.float32, jnp.bfloat16)],
        compiler_params=pltpu.CompilerParams(vmem_limit_bytes=24 << 20),
        cost_estimate=NO_COST,
        name="modulated_up",
    )(timesteps, places, table, up, *tokens)


def act_gradient(own, other, down, pre, rows):
    halves, total_rows, part = own.shape
    units, features = down.shape

    def kernel(down_ref, pre_ref, own_ref, other_ref, out_ref):
        total = jnp.zeros((rows, units), jnp.float32)
        for place in range(2 * halves):
            ref = (own_ref, other_ref)[place // halves]
            total = total + across(ref[place % halves], down_ref[:, place * part : (place + 1) * part])
        unused, pullback = jax.vjp(gelu_tanh, pre_ref[...])
        out_ref[...] = pullback(total)[0].astype(jnp.bfloat16)

    rows_of = pl.BlockSpec((halves, rows, part), lambda i: (0, i, 0))
    return pl.pallas_call(
        kernel,
        grid=(total_rows // rows,),
        in_specs=[
            pl.BlockSpec((units, features), lambda i: (0, 0)),
            pl.BlockSpec((rows, units), lambda i: (i, 0)),
            rows_of,
            rows_of,
        ],
        out_specs=pl.BlockSpec((rows, units), lambda i: (i, 0)),
        out_shape=jax.ShapeDtypeStruct((total_rows, units), jnp.bfloat16),
        compiler_params=pltpu.CompilerParams(vmem_limit_bytes=16 << 20),
        cost_estimate=NO_COST,
        name="act_gradient",
    )(down, pre, own, other)


def weight_gradient(own, other, right, steps, block, one_side, added=None):
    halves, _, part = own.shape
    units = right.shape[1]
    each = part // block
    count = halves * each
    half = block // 2
    kept = half if one_side else block
    skipped = half // LANES * LANES
    given = [own, other, right] + list(added or [])
    results, rows_out = (1, half) if one_side else (2, half)

    def kernel(step_ref, *refs):
        ins, outs = refs[: len(given)], refs[len(given) :]

        def keep(which, value):
            if added is None:
                outs[which][0] = value
                return
            value = (value + ins[3 + which][0]).astype(jnp.bfloat16)
            step = step_ref[which * count + pl.program_id(0)]
            for k, out in enumerate(outs):
                out[step] = value[k * rows_out : (k + 1) * rows_out]

        for which in range(2):
            if not one_side:
                keep(which, over_tokens(ins[which][0], ins[2][...]))
                continue

            @pl.when(step_ref[2 * count] == 0)
            def _():
                keep(which, over_tokens(ins[which][0, :, : block - skipped], ins[2][...])[:half])

            @pl.when(step_ref[2 * count] == 1)
            def _():
                keep(which, over_tokens(ins[which][0, :, skipped:], ins[2][...])[half - skipped :])

    block_of = pl.BlockSpec((1, kept, units), lambda i, step_ref: (i, 0, 0))
    in_specs = [pl.BlockSpec((1, own.shape[1], block), lambda i, step_ref: (i // each, 0, i % each))] * 2
    in_specs += [pl.BlockSpec(right.shape, lambda i, step_ref: (0, 0))] + [block_of] * (len(given) - 3)
    if added is None:
        out_specs, out_shape = [block_of] * 2, [jax.ShapeDtypeStruct((count, kept, units), jnp.float32)] * 2
    else:
        out_specs = [pl.BlockSpec((2 * count, rows_out, units), lambda i, step_ref: (0, 0, 0))] * results
        out_shape = [jax.ShapeDtypeStruct((2 * count, rows_out, units), jnp.bfloat16)] * results
    return pl.pallas_call(
        kernel,
        grid_spec=pltpu.PrefetchScalarGridSpec(
            num_scalar_prefetch=1, grid=(count,), in_specs=in_specs, out_specs=out_specs
        ),
        out_shape=out_shape,
        compiler_params=pltpu.CompilerParams(vmem_limit_bytes=20 << 20),
        cost_estimate=NO_COST,
        name="weight_gradient",
    )(steps, *given)


def after(x, *others):
    return lax.optimization_barrier((x, others))[0]


def received(arrivals):
    pieces, rows, share = arrivals[0].shape

    def kernel(*refs):
        for h, ref in enumerate(refs[:-1]):
            for k in range(pieces):
                refs[-1][h * rows : (h + 1) * rows, k * share : (k + 1) * share] = ref[k].astype(jnp.float32)

    return pl.pallas_call(
        kernel,
        out_shape=jax.ShapeDtypeStruct((rows * len(arrivals), pieces * share), jnp.float32),
        in_specs=in_vmem(len(arrivals)),
        out_specs=pl.BlockSpec(memory_space=pltpu.VMEM),
        compiler_params=pltpu.CompilerParams(vmem_limit_bytes=16 << 20),
        cost_estimate=NO_COST,
        name="received",
    )(*arrivals)


def partner(index, step, count):
    return index ^ step if count & (count - 1) == 0 else (step - index) % count


def shards(tokens, up_weight, down_weight, mod_table, timesteps, valid_counts):
    count, cores, sides = lax.axis_size("dp"), lax.axis_size("mp"), lax.axis_size("side")
    me, core, side = lax.axis_index("dp"), lax.axis_index("mp"), lax.axis_index("side")
    is_student = side == 1
    rows, width = tokens.shape
    pieces = 2 if width % (2 * LANES) == 0 and cores == 2 else 1
    part = width // pieces
    block, hidden = up_weight.shape[1:]
    share = hidden // count
    features = block * count
    first = core * width if cores == 2 else 0
    peers = [partner(me, step, count) for step in range(count)]
    feature_offsets = [(peer * block - first) % features for peer in peers]

    def sent(step, piece):
        pairs = [(i, partner(i, step, count)) for i in range(count)]
        return piece if all(i == j for i, j in pairs) else lax.ppermute(piece, "dp", pairs)

    wide = tokens.astype(jnp.float32)
    own_mean = jnp.mean(wide, axis=-1, keepdims=True)
    own_spread = jnp.sum((wide - own_mean) ** 2, axis=-1, keepdims=True)
    moments = jnp.concatenate([own_mean, own_spread], axis=1)
    if cores == 2:
        all_moments = jnp.stack([moments, from_core(moments, 1)])
    else:
        all_moments = lax.all_gather(moments, "mp")
    average = jnp.mean(all_moments[:, :, :1], axis=0)
    spread = jnp.sum(all_moments[:, :, 1:] + width * (all_moments[:, :, :1] - average) ** 2, axis=0)
    scaled = (wide - average) * lax.rsqrt(spread / features + 1e-06)
    modulation = lax.dynamic_slice(
        mod_table[0], (timesteps[0], 0, core * width), (1, mod_table.shape[2], width)
    )[0]
    normed = (scaled * (1.0 + modulation[1]) + modulation[0]).astype(jnp.bfloat16)
    gate = modulation[2]

    def own_features(array):
        return [ring_gather(array[:, c * part : (c + 1) * part], 1 if c % 2 == 0 else -1) for c in range(pieces)]

    def widened(found):
        own = stacked(found)
        if cores == 2:
            return [own, from_core(own, 1)]
        everything = lax.all_gather(own, "mp")
        return [everything[t] for t in range(cores)]

    def at(t, c):
        start = t * width + c * part
        return slice(start, start + part)

    parts = [(t, c) for t in range(cores) for c in range(pieces)]

    normed_found = own_features(normed)
    ups = [sent(k, lax.dynamic_slice_in_dim(up_weight[0], peers[k] * share, share, 1)) for k in range(count)]
    downs = []
    for k in range(count):
        piece = lax.dynamic_slice_in_dim(down_weight[0], peers[k] * share, share, 0)
        hop = min((k + 1) // 2, (count - 1) // 2)
        if k and hop:
            piece = after(piece, *[found[way] for found in normed_found for way in (hop, count - hop)])
        downs.append(sent(k, piece))
    up = placed_along(0, feature_offsets, ups, features)
    down = placed_along(1, feature_offsets, downs, features)

    all_normed = [widened(found) for found in normed_found]
    hidden_pre = sum(product(all_normed[c][t], up[at(t, c)]) for t, c in parts)
    hidden_act = gelu_tanh(hidden_pre).astype(jnp.bfloat16)

    valid_col = (jnp.arange(rows, dtype=jnp.int32) < valid_counts[me]).astype(jnp.float32)[:, None]
    valid_total = jnp.sum(valid_counts).astype(jnp.float32)

    def of_student(x):
        return jnp.where(is_student, x, lax.ppermute(x, "side", [(1, 0)]))

    student_gate = of_student(gate)
    student_act = of_student(hidden_act)

    outs, grads = [], []
    for c in range(pieces):
        if cores == 2:
            away = product(hidden_act, down[:, at(1, c)]).astype(jnp.bfloat16)
            term = product(hidden_act, down[:, at(0, c)]) + from_core(away, 1).astype(jnp.float32)
        else:
            term = lax.psum_scatter(
                product(hidden_act, down).astype(jnp.bfloat16), "mp", scatter_dimension=1, tiled=True
            ).astype(jnp.float32)
        mixed = ring_scatter([term[r * rows : (r + 1) * rows] for r in range(count)], 1 if c % 2 == 0 else -1)
        own = slice(c * part, (c + 1) * part)
        out = (wide[:, own] + gate[own] * mixed).astype(jnp.bfloat16)
        other = lax.ppermute(out, "side", [(0, 1), (1, 0)])
        differ = out.astype(jnp.float32) - other.astype(jnp.float32)
        differ = jnp.where(is_student, differ, -differ)
        grad = (student_gate[own] * differ * valid_col / jnp.sqrt(valid_total)).astype(jnp.bfloat16)
        outs.append(out)
        grads.append(grad)

    grads_found = lax.optimization_barrier(own_features(jnp.concatenate(grads, axis=1)))
    all_grads = [widened(found) for found in grads_found]

    def over_all_tokens(found, right):
        return jnp.concatenate([over_tokens(found[c][t], right).astype(jnp.bfloat16) for t, c in parts], axis=0)

    taken = block // sides

    def delivered(own):
        own = own.reshape(count * taken, share)
        arrivals = [
            sent(k, lax.dynamic_slice_in_dim(own, feature_offsets[k] // sides, taken, 0)) for k in range(count)
        ]
        result = jnp.zeros((taken, hidden), jnp.float32)
        for peer, piece in zip(peers, arrivals):
            result = lax.dynamic_update_slice_in_dim(result, piece.astype(jnp.float32), peer * share, 1)
        return result

    down_found = over_all_tokens(all_grads, student_act).reshape(count, sides, taken, share)
    down_share = delivered(lax.dynamic_index_in_dim(down_found, side, 1, keepdims=False))
    grad_act = sum(across(all_grads[c][t], down[:, at(t, c)]) for t, c in parts)
    unused, pullback = jax.vjp(gelu_tanh, hidden_pre)
    grad_pre = pullback(grad_act)[0].astype(jnp.bfloat16)
    if cores > 2:
        own_normed, grad_pre = lax.optimization_barrier((normed, grad_pre))
        all_normed = [widened(found) for found in own_features(own_normed)]
    up_found = over_all_tokens(all_normed, grad_pre).reshape(count, sides, taken, share)
    up_share = delivered(jnp.where(is_student, up_found[:, 1], lax.ppermute(up_found[:, 0], "side", [(1, 0)])))
    return (jnp.concatenate(outs, axis=1)[None], up_share, down_share.T)


def paired_shards(tokens, up_weight, down_weight, mod_table, timesteps, valid_counts):
    count = lax.axis_size("dp")
    me, core, side = lax.axis_index("dp"), lax.axis_index("mp"), lax.axis_index("side")
    is_student = side == 1
    rows, width = tokens.shape
    part = width // 2
    block, hidden = up_weight.shape[1:]
    share = hidden // count
    features = block * count
    taken = block // 2
    peers = [partner(me, step, count) for step in range(count)]
    swap = [(0, 1), (1, 0)]

    def feature_offset(owner):
        start = owner * block
        t, c = (start // width + core) % 2, (start // part % 2 + side) % 2
        return (2 * t + c) * part + start % part

    feature_offsets = [feature_offset(peer) for peer in peers]

    def sent(step, piece):
        pairs = [(i, partner(i, step, count)) for i in range(count)]
        return piece if all(i == j for i, j in pairs) else lax.ppermute(piece, "dp", pairs)

    def halves(array):
        return [lax.dynamic_slice_in_dim(array, ((side + c) % 2) * part, part, array.ndim - 1) for c in range(2)]

    def of_student(x):
        return jnp.where(is_student, x, lax.ppermute(x, "side", [(1, 0)]))

    part_places = jnp.stack([(core + t) % 2 * width + (side + c) % 2 * part for t in range(2) for c in range(2)])
    part_places = part_places.astype(jnp.int32)
    gate = lax.dynamic_slice(mod_table[0], (timesteps[0], 2, core * width), (1, 1, width)).reshape(width)
    gates = halves(gate)
    student_gate = of_student(gate)

    farthest = count // 2
    near_images = [0] + [r for hop in range(1, farthest - 1) for r in (hop, count - hop)]
    far_images = [farthest, farthest - 1, farthest + 1]
    steps = jnp.stack([part_places[p] // block + b for p in range(4) for b in range(part // block)])
    steps = jnp.concatenate([steps, side[None].astype(jnp.int32)])

    token_halves = halves(tokens)
    column = lax.broadcasted_iota(jnp.int32, (TILE_ROWS, part), 1)
    digits = jnp.where(column == 0, timesteps[0] % DIGIT, jnp.where(column == 1, timesteps[0] // DIGIT, 0))
    digits = digits.astype(jnp.bfloat16)
    there = back = jnp.concatenate([token_halves[0], digits], axis=0)
    round_ring = [there] + [None] * (count - 1)
    crossed = [jnp.concatenate([token_halves[1], digits], axis=0)]
    table = jnp.pad(mod_table[0], ((0, 0), (0, -mod_table.shape[2] % 8), (0, 0)))

    def cross_over(images):
        return lax.ppermute(stacked([round_ring[r] for r in images]), "side", swap)

    arrived = []
    for hop in range(1, farthest + 1):
        if hop == 2:
            there = after(there, table)
        if hop == farthest:
            there = after(there, crossed[1])
        there = ring_shift(there, 1)
        round_ring[-hop % count] = there
        if hop <= (count - 1) // 2:
            back = ring_shift(back, -1)
            round_ring[hop] = back
        arrived.append([there, back])
        if hop <= farthest - 2:
            crossed.append(cross_over([hop, count - hop]))
    far_crossed = cross_over(far_images)

    def exchanged(x):
        return lax.all_to_all(x, "dp", split_axis=0, concat_axis=0, tiled=True)

    up = exchanged(after(by_columns(up_weight[0], count), *arrived[-1]))
    down_blocks = exchanged(after(down_weight[0], up, crossed, far_crossed))

    def all_features(images, crossed):
        first = stacked([round_ring[r] for r in images])
        steps_taken = first.reshape(len(images), rows + TILE_ROWS, part)[:, rows, :2].astype(jnp.int32)
        pair = [first, crossed]
        shaped = [x.reshape(len(images), rows + TILE_ROWS, part) for x in pair + [from_core(x, 1) for x in pair]]
        return shaped, steps_taken[:, 0] + DIGIT * steps_taken[:, 1]

    near_tokens, near_steps = all_features(near_images, stacked(crossed))
    far_tokens, far_steps = all_features(far_images, far_crossed)
    *far_normed, far_pre, far_act = modulated_up(far_tokens, rows, far_steps, part_places, table, up)
    *near_normed, near_pre, near_act = modulated_up(near_tokens, rows, near_steps, part_places, table, up)

    def down_piece(k):
        return lambda refs, scalar_ref: refs[0].at[k * share : (k + 1) * share, :]

    offsets = [feature_offset(i) for i in range(count)]
    down = placed(1, offsets, [after(down_blocks, near_act, far_act)], [down_piece(k) for k in range(count)], (share, features))

    valid_col = (jnp.arange(rows, dtype=jnp.int32) < valid_counts[me]).astype(jnp.float32)[:, None]
    valid_total = jnp.sum(valid_counts).astype(jnp.float32)
    shares = {}

    def other_share(images, act):
        found = from_core(product(act, down[:, width:]).astype(jnp.bfloat16), 1)
        for k, r in enumerate(images):
            here = slice(k * rows, (k + 1) * rows)
            shares[r] = (act[here], found[here])
        return found

    def term(r, c):
        act, found = shares[r % count]
        here = slice(c * part, (c + 1) * part)
        return product(act, down[:, here]) + found[:, here].astype(jnp.float32)

    ways = (1, -1)
    far_share = other_share(far_images[:1], far_act[:rows])
    there = [ring_shift(term(farthest, c).astype(jnp.bfloat16), ways[c]) for c in range(2)]
    middle_share = other_share(far_images[1:], after(far_act[rows:], far_share))
    student_act = of_student(jnp.concatenate([near_act, far_act], axis=0))
    back = [None, None]
    other_share(near_images, after(near_act, middle_share))
    for hop in range(farthest - 1, 0, -1):
        if hop < farthest - 1:
            there = after(there, back)
        for c in range(2):
            there[c] = term(ways[c] * hop, c) + there[c].astype(jnp.float32)
            there[c] = ring_shift(there[c].astype(jnp.bfloat16), ways[c])
            value = term(-ways[c] * hop, c)
            value = value if back[c] is None else value + back[c].astype(jnp.float32)
            back[c] = ring_shift(value.astype(jnp.bfloat16), -ways[c])
    mixed = [term(0, c) + there[c].astype(jnp.float32) + back[c].astype(jnp.float32) for c in range(2)]
    mixed, student_act = lax.optimization_barrier((mixed, student_act))
    student_acts = [student_act[: len(near_images) * rows], student_act[len(near_images) * rows :]]
    student_gates = halves(student_gate)
    outs = [(token_halves[c].astype(jnp.float32) + gates[c] * mixed[c]).astype(jnp.bfloat16) for c in range(2)]
    found = []
    for c in range(2):
        differ = outs[c].astype(jnp.float32) - lax.ppermute(outs[1 - c], "side", swap).astype(jnp.float32)
        differ = jnp.where(is_student, differ, -differ)
        grad = (student_gates[c] * differ * valid_col / jnp.sqrt(valid_total)).astype(jnp.bfloat16)
        found.append([grad] + [None] * (count - 1))

    there, back = [found[c][0] for c in range(2)], [found[c][0] for c in range(2)]
    for hop in range(1, farthest + 1):
        if hop == 2:
            there = after(there, student_acts)
        if hop == farthest:
            near_own = stacked_parts([[found[c][r] for r in near_images] for c in range(2)])
            near_grads = [near_own, from_core(near_own, 1)]
            there = after(there, near_grads)
        for c, way in ((0, 1), (1, -1)):
            there[c] = ring_shift(there[c], way)
            found[c][(-way * hop) % count] = there[c]
            if hop <= (count - 1) // 2:
                back[c] = ring_shift(back[c], -way)
                found[c][(way * hop) % count] = back[c]
    near_grad_pre = act_gradient(*near_grads, down, near_pre, rows)
    far_found = [[found[c][r] for r in far_images] for c in range(2)]
    near_up = weight_gradient(*near_normed, near_grad_pre, steps, block, False)
    far_own = stacked_parts(after(far_found, *there, near_up))
    far_grads = [far_own, from_core(far_own, 1)]
    near_down = weight_gradient(*after(near_grads, far_own), student_acts[0], steps, block, True)

    def delivered(found):
        return exchanged(found.reshape(-1, share)).reshape(found.shape)

    (down_found,) = weight_gradient(*far_grads, student_acts[1], steps, block, True, near_down)
    down_arrived = delivered(down_found)
    far_grad_pre = act_gradient(*after(far_grads, down_found), down, far_pre, rows)
    up_found = weight_gradient(*far_normed, far_grad_pre, steps, block, False, near_up)
    handed = lax.ppermute(up_found[0], "side", [(1, 0)])
    up_arrived = [delivered(jnp.where(is_student, up_found[1], handed))]
    up_share, down_share = received(up_arrived), received([down_arrived])
    out = jnp.concatenate(
        [jnp.where(side == 0, outs[0], outs[1]), jnp.where(side == 0, outs[1], outs[0])], axis=1
    )
    return (out[None], up_share, down_share.T)


def solution(mesh):
    placed = (
        P("dp", "mp"),
        P("side", "dp", "mp"),
        P("side", "mp", "dp"),
        P("side", None, None, None),
        P("dp"),
        P(),
    )
    paired = mesh.shape["mp"] == mesh.shape["side"] == 2 and mesh.shape["dp"] in (8, 16, 32)
    return jax.shard_map(
        paired_shards if paired else shards,
        mesh=mesh,
        in_specs=placed,
        out_specs=(P("side", "dp", "mp"), P(("dp", "side"), "mp"), P("mp", ("dp", "side"))),
        check_vma=False,
    )
```

```python
import jax
import jax.numpy as jnp
from jax import lax
from jax.experimental import pallas as pl
from jax.experimental.pallas import tpu as pltpu
from jax.sharding import PartitionSpec as P

LANES = 128
TILE_ROWS = 16
DIGIT = 256


NO_COST = pl.CostEstimate(flops=1, bytes_accessed=1, transcendentals=0)


def cost(flops, bytes_accessed):
    return pl.CostEstimate(flops=flops, bytes_accessed=bytes_accessed, transcendentals=0)


def gelu_tanh(values):
    return jax.nn.gelu(values, approximate=True)


def product(left, right):
    return jnp.dot(left, right, preferred_element_type=jnp.float32)


def over_tokens(left, right):
    return lax.dot_general(left, right, (((0,), (0,)), ((), ())), preferred_element_type=jnp.float32)


def across(left, right):
    return lax.dot_general(left, right, (((1,), (1,)), ((), ())), preferred_element_type=jnp.float32)


def ring_order(count):
    return list(range(0, count, 2)) + list(range(1, count, 2))[::-1]


def ring_shift(x, by):
    order = ring_order(lax.axis_size("dp"))
    count = len(order)
    return lax.ppermute(x, "dp", [(order[p], order[(p + by) % count]) for p in range(count)])


def from_core(x, by):
    count = lax.axis_size("mp")
    return lax.ppermute(x, "mp", [((c + by) % count, c) for c in range(count)])


def ring_gather(x, sign):
    count = lax.axis_size("dp")
    found = [x] * count
    there = back = x
    for hop in range(1, count // 2 + 1):
        there = ring_shift(there, sign)
        found[(-sign * hop) % count] = there
        if hop <= (count - 1) // 2:
            back = ring_shift(back, -sign)
            found[(sign * hop) % count] = back
    return found


def ring_scatter(terms, sign):
    count = lax.axis_size("dp")
    total = terms[0]
    for way, hops in ((sign, count // 2), (-sign, (count - 1) // 2)):
        if hops:
            running = terms[(way * hops) % count]
            for hop in range(hops - 1, -1, -1):
                arrived = ring_shift(running.astype(jnp.bfloat16), way).astype(jnp.float32)
                if hop:
                    running = arrived + terms[(way * hop) % count]
                else:
                    total = total + arrived
    return total


def in_vmem(count):
    return [pl.BlockSpec(memory_space=pltpu.VMEM)] * count


def placed_along(axis, offsets, pieces, length):
    shape = list(pieces[0].shape)
    shape[axis] = length
    result = jnp.zeros(shape, pieces[0].dtype)
    for k, piece in enumerate(pieces):
        result = lax.dynamic_update_slice_in_dim(result, piece, offsets[k], axis)
    return result


def placed(axis, scalars, arrays, pieces, shape):
    count = len(pieces)

    def kernel(scalar_ref, *refs):
        *taken, result, semaphores = refs
        copies = []
        for k, piece in enumerate(pieces):
            source = piece(taken, scalar_ref)
            extent = source.shape[axis]
            where = pl.ds(pl.multiple_of(scalar_ref[k], extent), extent)
            target = result.at[where, :] if axis == 0 else result.at[:, where]
            copies.append(pltpu.make_async_copy(source, target, semaphores.at[k]))
            copies[-1].start()
        for copy in copies:
            copy.wait()

    return pl.pallas_call(
        kernel,
        out_shape=jax.ShapeDtypeStruct(shape, arrays[0].dtype),
        in_specs=[pl.BlockSpec(memory_space=pltpu.SMEM)] + [pl.BlockSpec(memory_space=pl.ANY)] * len(arrays),
        out_specs=pl.BlockSpec(memory_space=pltpu.VMEM),
        scratch_shapes=[pltpu.SemaphoreType.DMA((count,))],
        compiler_params=pltpu.CompilerParams(vmem_limit_bytes=16 << 20),
        cost_estimate=NO_COST,
        name="placed",
    )(jnp.stack(scalars).astype(jnp.int32), *arrays)


def by_columns(x, count):
    rows, columns = x.shape
    columns //= count

    def kernel(x_ref, result_ref):
        for k in range(count):
            result_ref[k * rows : (k + 1) * rows, :] = x_ref[:, k * columns : (k + 1) * columns]

    return pl.pallas_call(
        kernel,
        out_shape=jax.ShapeDtypeStruct((rows * count, columns), x.dtype),
        in_specs=in_vmem(1),
        out_specs=pl.BlockSpec(memory_space=pltpu.VMEM),
        compiler_params=pltpu.CompilerParams(vmem_limit_bytes=16 << 20),
        cost_estimate=NO_COST,
        name="by_columns",
    )(x)


def stacked(pieces):
    columns = pieces[0].shape[1]
    starts = [sum(piece.shape[0] for piece in pieces[:k]) for k in range(len(pieces) + 1)]
    if columns % LANES:
        return jnp.concatenate(pieces, axis=0)

    def kernel(*refs):
        for k, ref in enumerate(refs[:-1]):
            refs[-1][starts[k] : starts[k + 1], :] = ref[...]

    return pl.pallas_call(
        kernel,
        out_shape=jax.ShapeDtypeStruct((starts[-1], columns), pieces[0].dtype),
        in_specs=in_vmem(len(pieces)),
        out_specs=pl.BlockSpec(memory_space=pltpu.VMEM),
        compiler_params=pltpu.CompilerParams(vmem_limit_bytes=16 << 20),
        cost_estimate=NO_COST,
        name="stacked",
    )(*pieces)


def stacked_parts(parts):
    rows, columns = parts[0][0].shape
    count = len(parts[0])
    flat = [piece for pieces in parts for piece in pieces]

    def kernel(*refs):
        for k, ref in enumerate(refs[:-1]):
            at = k % count * rows
            refs[-1][k // count, at : at + rows, :] = ref[...]

    return pl.pallas_call(
        kernel,
        out_shape=jax.ShapeDtypeStruct((len(parts), rows * count, columns), parts[0][0].dtype),
        in_specs=in_vmem(len(flat)),
        out_specs=pl.BlockSpec(memory_space=pltpu.VMEM),
        compiler_params=pltpu.CompilerParams(vmem_limit_bytes=16 << 20),
        cost_estimate=NO_COST,
        name="stacked_parts",
    )(*flat)


def modulated_up(tokens, rows, timesteps, places, table, up):
    _, kinds, features = table.shape
    images = timesteps.shape[0]
    _, sent_rows, part = tokens[0].shape
    total_rows = images * rows
    units = up.shape[1]
    halves = len(tokens) // 2

    def kernel(step_ref, place_ref, table_ref, up_ref, *refs):
        taken, (own_out, other_out, pre_ref, act_ref) = refs[: 2 * halves], refs[2 * halves :]
        total = sum(jnp.sum(ref[0, :rows].astype(jnp.float32), axis=-1, keepdims=True) for ref in taken)
        average = total / features
        squares = sum(
            jnp.sum((ref[0, :rows].astype(jnp.float32) - average) ** 2, axis=-1, keepdims=True) for ref in taken
        )
        inverse = lax.rsqrt(squares / features + 1e-06)
        pre = jnp.zeros((rows, units), jnp.float32)
        for place, ref in enumerate(taken):
            scaled = (ref[0, :rows].astype(jnp.float32) - average) * inverse
            here = pl.ds(pl.multiple_of(place_ref[place], LANES), part)
            value = scaled * (1.0 + table_ref[0, 1:2, here]) + table_ref[0, 0:1, here]
            value = value.astype(jnp.bfloat16)
            (own_out, other_out)[place // halves][place % halves] = value
            pre = pre + jnp.dot(value, up_ref[here, :], preferred_element_type=jnp.float32)
        pre_ref[...] = pre
        act_ref[...] = gelu_tanh(pre).astype(jnp.bfloat16)

    rows_of = pl.BlockSpec((halves, rows, part), lambda i, step_ref, place_ref: (0, i, 0))
    units_of = pl.BlockSpec((rows, units), lambda i, step_ref, place_ref: (i, 0))
    return pl.pallas_call(
        kernel,
        grid_spec=pltpu.PrefetchScalarGridSpec(
            num_scalar_prefetch=2,
            grid=(images,),
            in_specs=[
                pl.BlockSpec((1, kinds, features), lambda i, step_ref, place_ref: (step_ref[i], 0, 0)),
                pl.BlockSpec((features, units), lambda i, step_ref, place_ref: (0, 0)),
            ]
            + [pl.BlockSpec((1, sent_rows, part), lambda i, step_ref, place_ref: (i, 0, 0))] * len(tokens),
            out_specs=[rows_of, rows_of, units_of, units_of],
        ),
        out_shape=[jax.ShapeDtypeStruct((halves, total_rows, part), jnp.bfloat16)] * 2
        + [jax.ShapeDtypeStruct((total_rows, units), kind) for kind in (jnp.float32, jnp.bfloat16)],
        compiler_params=pltpu.CompilerParams(vmem_limit_bytes=24 << 20),
        cost_estimate=cost(2 * total_rows * features * units, 4 * total_rows * features),
        name="modulated_up",
    )(timesteps, places, table, up, *tokens)


def act_gradient(own, other, down, pre, rows):
    halves, total_rows, part = own.shape
    units, features = down.shape

    def kernel(down_ref, pre_ref, own_ref, other_ref, out_ref):
        total = jnp.zeros((rows, units), jnp.float32)
        for place in range(2 * halves):
            ref = (own_ref, other_ref)[place // halves]
            total = total + across(ref[place % halves], down_ref[:, place * part : (place + 1) * part])
        unused, pullback = jax.vjp(gelu_tanh, pre_ref[...])
        out_ref[...] = pullback(total)[0].astype(jnp.bfloat16)

    rows_of = pl.BlockSpec((halves, rows, part), lambda i: (0, i, 0))
    return pl.pallas_call(
        kernel,
        grid=(total_rows // rows,),
        in_specs=[
            pl.BlockSpec((units, features), lambda i: (0, 0)),
            pl.BlockSpec((rows, units), lambda i: (i, 0)),
            rows_of,
            rows_of,
        ],
        out_specs=pl.BlockSpec((rows, units), lambda i: (i, 0)),
        out_shape=jax.ShapeDtypeStruct((total_rows, units), jnp.bfloat16),
        compiler_params=pltpu.CompilerParams(vmem_limit_bytes=16 << 20),
        cost_estimate=cost(2 * total_rows * features * units, 2 * total_rows * features),
        name="act_gradient",
    )(down, pre, own, other)


def weight_gradient(own, other, right, steps, block, added=None):
    halves, _, part = own.shape
    units = right.shape[1]
    each = part // block
    count = halves * each
    half = block // 2
    given = [own, other, right] + list(added or [])

    def kernel(step_ref, *refs):
        ins, outs = refs[: len(given)], refs[len(given) :]

        def keep(which, value):
            if added is None:
                outs[which][0] = value
                return
            value = (value + ins[3 + which][0]).astype(jnp.bfloat16)
            step = step_ref[which * count + pl.program_id(0)]
            for k, out in enumerate(outs):
                out[step] = value[k * half : (k + 1) * half]

        for which in range(2):
            keep(which, over_tokens(ins[which][0], ins[2][...]))

    block_of = pl.BlockSpec((1, block, units), lambda i, step_ref: (i, 0, 0))
    in_specs = [pl.BlockSpec((1, own.shape[1], block), lambda i, step_ref: (i // each, 0, i % each))] * 2
    in_specs += [pl.BlockSpec(right.shape, lambda i, step_ref: (0, 0))] + [block_of] * (len(given) - 3)
    if added is None:
        out_specs, out_shape = [block_of] * 2, [jax.ShapeDtypeStruct((count, block, units), jnp.float32)] * 2
    else:
        out_specs = [pl.BlockSpec((2 * count, half, units), lambda i, step_ref: (0, 0, 0))] * 2
        out_shape = [jax.ShapeDtypeStruct((2 * count, half, units), jnp.bfloat16)] * 2
    return pl.pallas_call(
        kernel,
        grid_spec=pltpu.PrefetchScalarGridSpec(
            num_scalar_prefetch=1, grid=(count,), in_specs=in_specs, out_specs=out_specs
        ),
        out_shape=out_shape,
        compiler_params=pltpu.CompilerParams(vmem_limit_bytes=20 << 20),
        cost_estimate=cost(4 * own.size * units, 4 * own.size),
        name="weight_gradient",
    )(steps, *given)


def side_gradient(lefts, rights, steps, block):
    halves, _, part = lefts[0][0].shape
    units = rights[0].shape[1]
    each = part // block
    count = halves * each
    half = block // 2
    groups = len(lefts)
    skipped = half // LANES * LANES

    def kernel(step_ref, *refs):
        left_refs, right_refs, out_ref = refs[: 2 * groups], refs[2 * groups : 3 * groups], refs[-1]

        def found(which, begin, end):
            return sum(
                over_tokens(left_refs[2 * g + which][0, :, begin:end], right_refs[g][...]) for g in range(groups)
            ).astype(jnp.bfloat16)

        for which in range(2):
            step = step_ref[which * count + pl.program_id(0)]

            @pl.when(step_ref[2 * count] == 0)
            def _():
                out_ref[step] = found(which, 0, block - skipped)[:half]

            @pl.when(step_ref[2 * count] == 1)
            def _():
                out_ref[step] = found(which, skipped, block)[half - skipped :]

    left_specs = [
        pl.BlockSpec((1, x.shape[1], block), lambda i, step_ref: (i // each, 0, i % each)) for pair in lefts for x in pair
    ]
    right_specs = [pl.BlockSpec(x.shape, lambda i, step_ref: (0, 0)) for x in rights]
    return pl.pallas_call(
        kernel,
        grid_spec=pltpu.PrefetchScalarGridSpec(
            num_scalar_prefetch=1,
            grid=(count,),
            in_specs=left_specs + right_specs,
            out_specs=pl.BlockSpec((2 * count, half, units), lambda i, step_ref: (0, 0, 0)),
        ),
        out_shape=jax.ShapeDtypeStruct((2 * count, half, units), jnp.bfloat16),
        compiler_params=pltpu.CompilerParams(vmem_limit_bytes=24 << 20),
        cost_estimate=cost(4 * sum(x.size for x in rights) * halves * part, 4 * sum(x.shape[0] for x in rights) * halves * part),
        name="side_gradient",
    )(steps, *[x for pair in lefts for x in pair], *rights)


def after(x, *others):
    return lax.optimization_barrier((x, others))[0]


def received(arrivals):
    pieces, rows, share = arrivals[0].shape

    def kernel(*refs):
        for h, ref in enumerate(refs[:-1]):
            for k in range(pieces):
                refs[-1][h * rows : (h + 1) * rows, k * share : (k + 1) * share] = ref[k].astype(jnp.float32)

    return pl.pallas_call(
        kernel,
        out_shape=jax.ShapeDtypeStruct((rows * len(arrivals), pieces * share), jnp.float32),
        in_specs=in_vmem(len(arrivals)),
        out_specs=pl.BlockSpec(memory_space=pltpu.VMEM),
        compiler_params=pltpu.CompilerParams(vmem_limit_bytes=16 << 20),
        cost_estimate=NO_COST,
        name="received",
    )(*arrivals)


def partner(index, step, count):
    return index ^ step if count & (count - 1) == 0 else (step - index) % count


def shards(tokens, up_weight, down_weight, mod_table, timesteps, valid_counts):
    count, cores, sides = lax.axis_size("dp"), lax.axis_size("mp"), lax.axis_size("side")
    me, core, side = lax.axis_index("dp"), lax.axis_index("mp"), lax.axis_index("side")
    is_student = side == 1
    rows, width = tokens.shape
    pieces = 2 if width % (2 * LANES) == 0 and cores == 2 else 1
    part = width // pieces
    block, hidden = up_weight.shape[1:]
    share = hidden // count
    features = block * count
    first = core * width if cores == 2 else 0
    peers = [partner(me, step, count) for step in range(count)]
    feature_offsets = [(peer * block - first) % features for peer in peers]

    def sent(step, piece):
        pairs = [(i, partner(i, step, count)) for i in range(count)]
        return piece if all(i == j for i, j in pairs) else lax.ppermute(piece, "dp", pairs)

    wide = tokens.astype(jnp.float32)
    own_mean = jnp.mean(wide, axis=-1, keepdims=True)
    own_spread = jnp.sum((wide - own_mean) ** 2, axis=-1, keepdims=True)
    moments = jnp.concatenate([own_mean, own_spread], axis=1)
    if cores == 2:
        all_moments = jnp.stack([moments, from_core(moments, 1)])
    else:
        all_moments = lax.all_gather(moments, "mp")
    average = jnp.mean(all_moments[:, :, :1], axis=0)
    spread = jnp.sum(all_moments[:, :, 1:] + width * (all_moments[:, :, :1] - average) ** 2, axis=0)
    scaled = (wide - average) * lax.rsqrt(spread / features + 1e-06)
    modulation = lax.dynamic_slice(
        mod_table[0], (timesteps[0], 0, core * width), (1, mod_table.shape[2], width)
    )[0]
    normed = (scaled * (1.0 + modulation[1]) + modulation[0]).astype(jnp.bfloat16)
    gate = modulation[2]

    def own_features(array):
        return [ring_gather(array[:, c * part : (c + 1) * part], 1 if c % 2 == 0 else -1) for c in range(pieces)]

    def widened(found):
        own = stacked(found)
        if cores == 2:
            return [own, from_core(own, 1)]
        everything = lax.all_gather(own, "mp")
        return [everything[t] for t in range(cores)]

    def at(t, c):
        start = t * width + c * part
        return slice(start, start + part)

    parts = [(t, c) for t in range(cores) for c in range(pieces)]

    normed_found = own_features(normed)
    ups = [sent(k, lax.dynamic_slice_in_dim(up_weight[0], peers[k] * share, share, 1)) for k in range(count)]
    downs = []
    for k in range(count):
        piece = lax.dynamic_slice_in_dim(down_weight[0], peers[k] * share, share, 0)
        hop = min((k + 1) // 2, (count - 1) // 2)
        if k and hop:
            piece = after(piece, *[found[way] for found in normed_found for way in (hop, count - hop)])
        downs.append(sent(k, piece))
    up = placed_along(0, feature_offsets, ups, features)
    down = placed_along(1, feature_offsets, downs, features)

    all_normed = [widened(found) for found in normed_found]
    hidden_pre = sum(product(all_normed[c][t], up[at(t, c)]) for t, c in parts)
    hidden_act = gelu_tanh(hidden_pre).astype(jnp.bfloat16)

    valid_col = (jnp.arange(rows, dtype=jnp.int32) < valid_counts[me]).astype(jnp.float32)[:, None]
    valid_total = jnp.sum(valid_counts).astype(jnp.float32)

    def of_student(x):
        return jnp.where(is_student, x, lax.ppermute(x, "side", [(1, 0)]))

    student_gate = of_student(gate)
    student_act = of_student(hidden_act)

    outs, grads = [], []
    for c in range(pieces):
        if cores == 2:
            away = product(hidden_act, down[:, at(1, c)]).astype(jnp.bfloat16)
            term = product(hidden_act, down[:, at(0, c)]) + from_core(away, 1).astype(jnp.float32)
        else:
            term = lax.psum_scatter(
                product(hidden_act, down).astype(jnp.bfloat16), "mp", scatter_dimension=1, tiled=True
            ).astype(jnp.float32)
        mixed = ring_scatter([term[r * rows : (r + 1) * rows] for r in range(count)], 1 if c % 2 == 0 else -1)
        own = slice(c * part, (c + 1) * part)
        out = (wide[:, own] + gate[own] * mixed).astype(jnp.bfloat16)
        other = lax.ppermute(out, "side", [(0, 1), (1, 0)])
        differ = out.astype(jnp.float32) - other.astype(jnp.float32)
        differ = jnp.where(is_student, differ, -differ)
        grad = (student_gate[own] * differ * valid_col / jnp.sqrt(valid_total)).astype(jnp.bfloat16)
        outs.append(out)
        grads.append(grad)

    grads_found = lax.optimization_barrier(own_features(jnp.concatenate(grads, axis=1)))
    all_grads = [widened(found) for found in grads_found]

    def over_all_tokens(found, right):
        return jnp.concatenate([over_tokens(found[c][t], right).astype(jnp.bfloat16) for t, c in parts], axis=0)

    taken = block // sides

    def delivered(own):
        own = own.reshape(count * taken, share)
        arrivals = [
            sent(k, lax.dynamic_slice_in_dim(own, feature_offsets[k] // sides, taken, 0)) for k in range(count)
        ]
        result = jnp.zeros((taken, hidden), jnp.float32)
        for peer, piece in zip(peers, arrivals):
            result = lax.dynamic_update_slice_in_dim(result, piece.astype(jnp.float32), peer * share, 1)
        return result

    down_found = over_all_tokens(all_grads, student_act).reshape(count, sides, taken, share)
    down_share = delivered(lax.dynamic_index_in_dim(down_found, side, 1, keepdims=False))
    grad_act = sum(across(all_grads[c][t], down[:, at(t, c)]) for t, c in parts)
    unused, pullback = jax.vjp(gelu_tanh, hidden_pre)
    grad_pre = pullback(grad_act)[0].astype(jnp.bfloat16)
    if cores > 2:
        own_normed, grad_pre = lax.optimization_barrier((normed, grad_pre))
        all_normed = [widened(found) for found in own_features(own_normed)]
    up_found = over_all_tokens(all_normed, grad_pre).reshape(count, sides, taken, share)
    up_share = delivered(jnp.where(is_student, up_found[:, 1], lax.ppermute(up_found[:, 0], "side", [(1, 0)])))
    return (jnp.concatenate(outs, axis=1)[None], up_share, down_share.T)


def paired_shards(tokens, up_weight, down_weight, mod_table, timesteps, valid_counts):
    count = lax.axis_size("dp")
    me, core, side = lax.axis_index("dp"), lax.axis_index("mp"), lax.axis_index("side")
    is_student = side == 1
    rows, width = tokens.shape
    part = width // 2
    block, hidden = up_weight.shape[1:]
    share = hidden // count
    features = block * count
    taken = block // 2
    peers = [partner(me, step, count) for step in range(count)]
    swap = [(0, 1), (1, 0)]

    def feature_offset(owner):
        start = owner * block
        t, c = (start // width + core) % 2, (start // part % 2 + side) % 2
        return (2 * t + c) * part + start % part

    feature_offsets = [feature_offset(peer) for peer in peers]

    def sent(step, piece):
        pairs = [(i, partner(i, step, count)) for i in range(count)]
        return piece if all(i == j for i, j in pairs) else lax.ppermute(piece, "dp", pairs)

    def halves(array):
        return [lax.dynamic_slice_in_dim(array, ((side + c) % 2) * part, part, array.ndim - 1) for c in range(2)]

    def of_student(x):
        return jnp.where(is_student, x, lax.ppermute(x, "side", [(1, 0)]))

    part_places = jnp.stack([(core + t) % 2 * width + (side + c) % 2 * part for t in range(2) for c in range(2)])
    part_places = part_places.astype(jnp.int32)
    gate = lax.dynamic_slice(mod_table[0], (timesteps[0], 2, core * width), (1, 1, width)).reshape(width)
    gates = halves(gate)
    student_gate = of_student(gate)

    farthest = count // 2
    near_images = [0] + [r for hop in range(1, farthest - 1) for r in (hop, count - hop)]
    far_images = [farthest, farthest - 1, farthest + 1]
    steps = jnp.stack([part_places[p] // block + b for p in range(4) for b in range(part // block)])
    steps = jnp.concatenate([steps, side[None].astype(jnp.int32)])

    token_halves = halves(tokens)
    column = lax.broadcasted_iota(jnp.int32, (TILE_ROWS, part), 1)
    digits = jnp.where(column == 0, timesteps[0] % DIGIT, jnp.where(column == 1, timesteps[0] // DIGIT, 0))
    digits = digits.astype(jnp.bfloat16)
    there = back = jnp.concatenate([token_halves[0], digits], axis=0)
    round_ring = [there] + [None] * (count - 1)
    crossed = [jnp.concatenate([token_halves[1], digits], axis=0)]
    table = jnp.pad(mod_table[0], ((0, 0), (0, -mod_table.shape[2] % 8), (0, 0)))

    def cross_over(images):
        return lax.ppermute(stacked([round_ring[r] for r in images]), "side", swap)

    arrived = []
    for hop in range(1, farthest + 1):
        if hop == 2:
            there = after(there, table)
        if hop == farthest:
            there = after(there, crossed[1])
        there = ring_shift(there, 1)
        round_ring[-hop % count] = there
        if hop <= (count - 1) // 2:
            back = ring_shift(back, -1)
            round_ring[hop] = back
        arrived.append([there, back])
        if hop <= farthest - 2:
            crossed.append(cross_over([hop, count - hop]))
    far_crossed = cross_over(far_images)

    def exchanged(x):
        return lax.all_to_all(x, "dp", split_axis=0, concat_axis=0, tiled=True)

    up = exchanged(after(by_columns(up_weight[0], count), *arrived[-1]))
    down_blocks = exchanged(after(down_weight[0], up, crossed, far_crossed))

    def all_features(images, crossed):
        first = stacked([round_ring[r] for r in images])
        steps_taken = first.reshape(len(images), rows + TILE_ROWS, part)[:, rows, :2].astype(jnp.int32)
        pair = [first, crossed]
        shaped = [x.reshape(len(images), rows + TILE_ROWS, part) for x in pair + [from_core(x, 1) for x in pair]]
        return shaped, steps_taken[:, 0] + DIGIT * steps_taken[:, 1]

    near_tokens, near_steps = all_features(near_images, stacked(crossed))
    far_tokens, far_steps = all_features(far_images, far_crossed)
    *far_normed, far_pre, far_act = modulated_up(far_tokens, rows, far_steps, part_places, table, up)
    *near_normed, near_pre, near_act = modulated_up(near_tokens, rows, near_steps, part_places, table, up)

    def down_piece(k):
        return lambda refs, scalar_ref: refs[0].at[k * share : (k + 1) * share, :]

    offsets = [feature_offset(i) for i in range(count)]
    down = placed(1, offsets, [after(down_blocks, near_act, far_act)], [down_piece(k) for k in range(count)], (share, features))

    valid_col = (jnp.arange(rows, dtype=jnp.int32) < valid_counts[me]).astype(jnp.float32)[:, None]
    valid_total = jnp.sum(valid_counts).astype(jnp.float32)
    shares = {}

    def other_share(images, act):
        found = from_core(product(act, down[:, width:]).astype(jnp.bfloat16), 1)
        for k, r in enumerate(images):
            here = slice(k * rows, (k + 1) * rows)
            shares[r] = (act[here], found[here])
        return found

    def term(r, c):
        act, found = shares[r % count]
        here = slice(c * part, (c + 1) * part)
        return product(act, down[:, here]) + found[:, here].astype(jnp.float32)

    ways = (1, -1)
    far_share = other_share(far_images[:1], far_act[:rows])
    there = [ring_shift(term(farthest, c).astype(jnp.bfloat16), ways[c]) for c in range(2)]
    other_share(far_images[1:], after(far_act[rows:], far_share))
    student_act = of_student(jnp.concatenate([near_act, far_act], axis=0))
    back = [None, None]
    other_share(near_images, after(near_act, far_share))
    for hop in range(farthest - 1, 0, -1):
        if hop < farthest - 1:
            there = after(there, back)
        for c in range(2):
            there[c] = term(ways[c] * hop, c) + there[c].astype(jnp.float32)
            there[c] = ring_shift(there[c].astype(jnp.bfloat16), ways[c])
            value = term(-ways[c] * hop, c)
            value = value if back[c] is None else value + back[c].astype(jnp.float32)
            back[c] = ring_shift(value.astype(jnp.bfloat16), -ways[c])
    mixed = [term(0, c) + there[c].astype(jnp.float32) + back[c].astype(jnp.float32) for c in range(2)]
    mixed, student_act = lax.optimization_barrier((mixed, student_act))
    student_acts = [student_act[: len(near_images) * rows], student_act[len(near_images) * rows :]]
    student_gates = halves(student_gate)
    outs = [(token_halves[c].astype(jnp.float32) + gates[c] * mixed[c]).astype(jnp.bfloat16) for c in range(2)]
    found = []
    for c in range(2):
        differ = outs[c].astype(jnp.float32) - lax.ppermute(outs[1 - c], "side", swap).astype(jnp.float32)
        differ = jnp.where(is_student, differ, -differ)
        grad = (student_gates[c] * differ * valid_col / jnp.sqrt(valid_total)).astype(jnp.bfloat16)
        found.append([grad] + [None] * (count - 1))

    there, back = [found[c][0] for c in range(2)], [found[c][0] for c in range(2)]
    for hop in range(1, farthest + 1):
        if hop == 2:
            there = after(there, student_acts)
        if hop == farthest:
            near_own = stacked_parts([[found[c][r] for r in near_images] for c in range(2)])
            near_grads = [near_own, from_core(near_own, 1)]
            there = after(there, near_grads)
        for c, way in ((0, 1), (1, -1)):
            there[c] = ring_shift(there[c], way)
            found[c][(-way * hop) % count] = there[c]
            if hop <= (count - 1) // 2:
                back[c] = ring_shift(back[c], -way)
                found[c][(way * hop) % count] = back[c]
    near_grad_pre = act_gradient(*near_grads, down, near_pre, rows)
    far_found = [[found[c][r] for r in far_images] for c in range(2)]
    near_up = weight_gradient(*near_normed, near_grad_pre, steps, block)
    far_own = stacked_parts(after(far_found, *there, near_up))
    far_grads = [far_own, from_core(far_own, 1)]

    def delivered(found):
        return exchanged(found.reshape(-1, share)).reshape(found.shape)

    far_grad_pre = act_gradient(*far_grads, down, far_pre, rows)
    up_found = weight_gradient(*far_normed, far_grad_pre, steps, block, near_up)
    far_grads = after(far_grads, up_found)
    down_found = side_gradient([near_grads, far_grads], student_acts, steps, block)
    down_arrived = delivered(down_found)
    handed = lax.ppermute(up_found[0], "side", [(1, 0)])
    up_arrived = [delivered(jnp.where(is_student, up_found[1], handed))]
    up_share, down_share = received(up_arrived), received([down_arrived])
    out = jnp.concatenate(
        [jnp.where(side == 0, outs[0], outs[1]), jnp.where(side == 0, outs[1], outs[0])], axis=1
    )
    return (out[None], up_share, down_share.T)


def solution(mesh):
    placed = (
        P("dp", "mp"),
        P("side", "dp", "mp"),
        P("side", "mp", "dp"),
        P("side", None, None, None),
        P("dp"),
        P(),
    )
    paired = mesh.shape["mp"] == mesh.shape["side"] == 2 and mesh.shape["dp"] in (8, 16, 32)
    return jax.shard_map(
        paired_shards if paired else shards,
        mesh=mesh,
        in_specs=placed,
        out_specs=(P("side", "dp", "mp"), P(("dp", "side"), "mp"), P("mp", ("dp", "side"))),
        check_vma=False,
    )
```

```python
import jax
import jax.numpy as jnp
from jax import lax
from jax.experimental import pallas as pl
from jax.experimental.pallas import tpu as pltpu
from jax.sharding import PartitionSpec as P

LANES = 128
TILE_ROWS = 16
DIGIT = 256


NO_COST = pl.CostEstimate(flops=1, bytes_accessed=1, transcendentals=0)


def cost(flops, bytes_accessed):
    return pl.CostEstimate(flops=flops, bytes_accessed=bytes_accessed, transcendentals=0)


def gelu_tanh(values):
    return jax.nn.gelu(values, approximate=True)


def product(left, right):
    return jnp.dot(left, right, preferred_element_type=jnp.float32)


def over_tokens(left, right):
    return lax.dot_general(left, right, (((0,), (0,)), ((), ())), preferred_element_type=jnp.float32)


def across(left, right):
    return lax.dot_general(left, right, (((1,), (1,)), ((), ())), preferred_element_type=jnp.float32)


def ring_order(count):
    return list(range(0, count, 2)) + list(range(1, count, 2))[::-1]


def ring_shift(x, by):
    order = ring_order(lax.axis_size("dp"))
    count = len(order)
    return lax.ppermute(x, "dp", [(order[p], order[(p + by) % count]) for p in range(count)])


def from_core(x, by):
    count = lax.axis_size("mp")
    return lax.ppermute(x, "mp", [((c + by) % count, c) for c in range(count)])


def ring_gather(x, sign):
    count = lax.axis_size("dp")
    found = [x] * count
    there = back = x
    for hop in range(1, count // 2 + 1):
        there = ring_shift(there, sign)
        found[(-sign * hop) % count] = there
        if hop <= (count - 1) // 2:
            back = ring_shift(back, -sign)
            found[(sign * hop) % count] = back
    return found


def ring_scatter(terms, sign):
    count = lax.axis_size("dp")
    total = terms[0]
    for way, hops in ((sign, count // 2), (-sign, (count - 1) // 2)):
        if hops:
            running = terms[(way * hops) % count]
            for hop in range(hops - 1, -1, -1):
                arrived = ring_shift(running.astype(jnp.bfloat16), way).astype(jnp.float32)
                if hop:
                    running = arrived + terms[(way * hop) % count]
                else:
                    total = total + arrived
    return total


def in_vmem(count):
    return [pl.BlockSpec(memory_space=pltpu.VMEM)] * count


def placed_along(axis, offsets, pieces, length):
    shape = list(pieces[0].shape)
    shape[axis] = length
    result = jnp.zeros(shape, pieces[0].dtype)
    for k, piece in enumerate(pieces):
        result = lax.dynamic_update_slice_in_dim(result, piece, offsets[k], axis)
    return result


def placed(axis, scalars, arrays, pieces, shape):
    count = len(pieces)

    def kernel(scalar_ref, *refs):
        *taken, result, semaphores = refs
        copies = []
        for k, piece in enumerate(pieces):
            source = piece(taken, scalar_ref)
            extent = source.shape[axis]
            where = pl.ds(pl.multiple_of(scalar_ref[k], extent), extent)
            target = result.at[where, :] if axis == 0 else result.at[:, where]
            copies.append(pltpu.make_async_copy(source, target, semaphores.at[k]))
            copies[-1].start()
        for copy in copies:
            copy.wait()

    return pl.pallas_call(
        kernel,
        out_shape=jax.ShapeDtypeStruct(shape, arrays[0].dtype),
        in_specs=[pl.BlockSpec(memory_space=pltpu.SMEM)] + [pl.BlockSpec(memory_space=pl.ANY)] * len(arrays),
        out_specs=pl.BlockSpec(memory_space=pltpu.VMEM),
        scratch_shapes=[pltpu.SemaphoreType.DMA((count,))],
        compiler_params=pltpu.CompilerParams(vmem_limit_bytes=16 << 20),
        cost_estimate=NO_COST,
        name="placed",
    )(jnp.stack(scalars).astype(jnp.int32), *arrays)


def by_columns(x, count):
    rows, columns = x.shape
    columns //= count

    def kernel(x_ref, result_ref):
        for k in range(count):
            result_ref[k * rows : (k + 1) * rows, :] = x_ref[:, k * columns : (k + 1) * columns]

    return pl.pallas_call(
        kernel,
        out_shape=jax.ShapeDtypeStruct((rows * count, columns), x.dtype),
        in_specs=in_vmem(1),
        out_specs=pl.BlockSpec(memory_space=pltpu.VMEM),
        compiler_params=pltpu.CompilerParams(vmem_limit_bytes=16 << 20),
        cost_estimate=NO_COST,
        name="by_columns",
    )(x)


def stacked(pieces):
    columns = pieces[0].shape[1]
    starts = [sum(piece.shape[0] for piece in pieces[:k]) for k in range(len(pieces) + 1)]
    if columns % LANES:
        return jnp.concatenate(pieces, axis=0)

    def kernel(*refs):
        for k, ref in enumerate(refs[:-1]):
            refs[-1][starts[k] : starts[k + 1], :] = ref[...]

    return pl.pallas_call(
        kernel,
        out_shape=jax.ShapeDtypeStruct((starts[-1], columns), pieces[0].dtype),
        in_specs=in_vmem(len(pieces)),
        out_specs=pl.BlockSpec(memory_space=pltpu.VMEM),
        compiler_params=pltpu.CompilerParams(vmem_limit_bytes=16 << 20),
        cost_estimate=NO_COST,
        name="stacked",
    )(*pieces)


def stacked_parts(parts):
    rows, columns = parts[0][0].shape
    count = len(parts[0])
    flat = [piece for pieces in parts for piece in pieces]

    def kernel(*refs):
        for k, ref in enumerate(refs[:-1]):
            at = k % count * rows
            refs[-1][k // count, at : at + rows, :] = ref[...]

    return pl.pallas_call(
        kernel,
        out_shape=jax.ShapeDtypeStruct((len(parts), rows * count, columns), parts[0][0].dtype),
        in_specs=in_vmem(len(flat)),
        out_specs=pl.BlockSpec(memory_space=pltpu.VMEM),
        compiler_params=pltpu.CompilerParams(vmem_limit_bytes=16 << 20),
        cost_estimate=NO_COST,
        name="stacked_parts",
    )(*flat)


def modulated_up(tokens, rows, timesteps, places, table, up):
    _, kinds, features = table.shape
    images = timesteps.shape[0]
    _, sent_rows, part = tokens[0].shape
    total_rows = images * rows
    units = up.shape[1]
    halves = len(tokens) // 2

    def kernel(step_ref, place_ref, table_ref, up_ref, *refs):
        taken, (own_out, other_out, pre_ref, act_ref) = refs[: 2 * halves], refs[2 * halves :]
        total = sum(jnp.sum(ref[0, :rows].astype(jnp.float32), axis=-1, keepdims=True) for ref in taken)
        average = total / features
        squares = sum(
            jnp.sum((ref[0, :rows].astype(jnp.float32) - average) ** 2, axis=-1, keepdims=True) for ref in taken
        )
        inverse = lax.rsqrt(squares / features + 1e-06)
        pre = jnp.zeros((rows, units), jnp.float32)
        for place, ref in enumerate(taken):
            scaled = (ref[0, :rows].astype(jnp.float32) - average) * inverse
            here = pl.ds(pl.multiple_of(place_ref[place], LANES), part)
            value = scaled * (1.0 + table_ref[0, 1:2, here]) + table_ref[0, 0:1, here]
            value = value.astype(jnp.bfloat16)
            (own_out, other_out)[place // halves][place % halves] = value
            pre = pre + jnp.dot(value, up_ref[here, :], preferred_element_type=jnp.float32)
        pre_ref[...] = pre
        act_ref[...] = gelu_tanh(pre).astype(jnp.bfloat16)

    rows_of = pl.BlockSpec((halves, rows, part), lambda i, step_ref, place_ref: (0, i, 0))
    units_of = pl.BlockSpec((rows, units), lambda i, step_ref, place_ref: (i, 0))
    return pl.pallas_call(
        kernel,
        grid_spec=pltpu.PrefetchScalarGridSpec(
            num_scalar_prefetch=2,
            grid=(images,),
            in_specs=[
                pl.BlockSpec((1, kinds, features), lambda i, step_ref, place_ref: (step_ref[i], 0, 0)),
                pl.BlockSpec((features, units), lambda i, step_ref, place_ref: (0, 0)),
            ]
            + [pl.BlockSpec((1, sent_rows, part), lambda i, step_ref, place_ref: (i, 0, 0))] * len(tokens),
            out_specs=[rows_of, rows_of, units_of, units_of],
        ),
        out_shape=[jax.ShapeDtypeStruct((halves, total_rows, part), jnp.bfloat16)] * 2
        + [jax.ShapeDtypeStruct((total_rows, units), kind) for kind in (jnp.float32, jnp.bfloat16)],
        compiler_params=pltpu.CompilerParams(vmem_limit_bytes=24 << 20),
        cost_estimate=cost(2 * total_rows * features * units, 4 * total_rows * features),
        name="modulated_up",
    )(timesteps, places, table, up, *tokens)


def act_gradient(own, other, down, pre, rows):
    halves, total_rows, part = own.shape
    units, features = down.shape

    def kernel(down_ref, pre_ref, own_ref, other_ref, out_ref):
        total = jnp.zeros((rows, units), jnp.float32)
        for place in range(2 * halves):
            ref = (own_ref, other_ref)[place // halves]
            total = total + across(ref[place % halves], down_ref[:, place * part : (place + 1) * part])
        unused, pullback = jax.vjp(gelu_tanh, pre_ref[...])
        out_ref[...] = pullback(total)[0].astype(jnp.bfloat16)

    rows_of = pl.BlockSpec((halves, rows, part), lambda i: (0, i, 0))
    return pl.pallas_call(
        kernel,
        grid=(total_rows // rows,),
        in_specs=[
            pl.BlockSpec((units, features), lambda i: (0, 0)),
            pl.BlockSpec((rows, units), lambda i: (i, 0)),
            rows_of,
            rows_of,
        ],
        out_specs=pl.BlockSpec((rows, units), lambda i: (i, 0)),
        out_shape=jax.ShapeDtypeStruct((total_rows, units), jnp.bfloat16),
        compiler_params=pltpu.CompilerParams(vmem_limit_bytes=16 << 20),
        cost_estimate=cost(2 * total_rows * features * units, 2 * total_rows * features),
        name="act_gradient",
    )(down, pre, own, other)


def weight_gradient(own, other, right, steps, block, added=None):
    halves, _, part = own.shape
    units = right.shape[1]
    each = part // block
    count = halves * each
    half = block // 2
    given = [own, other, right] + list(added or [])

    def kernel(step_ref, *refs):
        ins, outs = refs[: len(given)], refs[len(given) :]
        for b in range(count):
            here = slice(b % each * block, (b % each + 1) * block)
            for which in range(2):
                value = over_tokens(ins[which][b // each, :, here], ins[2][...])
                if added is None:
                    outs[which][b] = value
                    continue
                value = (value + ins[3 + which][b]).astype(jnp.bfloat16)
                step = step_ref[which * count + b]
                for k, out in enumerate(outs):
                    out[step] = value[k * half : (k + 1) * half]

    shape, kind = ((count, block, units), jnp.float32) if added is None else ((2 * count, half, units), jnp.bfloat16)
    return pl.pallas_call(
        kernel,
        in_specs=[pl.BlockSpec(memory_space=pltpu.SMEM)] + in_vmem(len(given)),
        out_specs=in_vmem(2),
        out_shape=[jax.ShapeDtypeStruct(shape, kind)] * 2,
        compiler_params=pltpu.CompilerParams(vmem_limit_bytes=28 << 20),
        cost_estimate=cost(4 * own.size * units, 4 * own.size),
        name="weight_gradient",
    )(steps, *given)


def side_gradient(lefts, rights, steps, first, block, base=None):
    halves, _, part = lefts[0].shape
    units = rights[0].shape[1]
    each = part // block
    count = halves * each
    half = block // 2
    groups = len(lefts)
    skipped = half // LANES * LANES
    bases = [] if base is None else [base]

    def kernel(step_ref, *refs):
        left_refs, right_refs, out_ref = refs[:groups], refs[groups : 2 * groups], refs[-1]

        if bases:

            @pl.when(pl.program_id(0) == 0)
            def _():
                out_ref[...] = refs[2 * groups][...]

        def found(begin, end):
            return sum(
                over_tokens(left_refs[g][0, :, begin:end], right_refs[g][...]) for g in range(groups)
            ).astype(jnp.bfloat16)

        step = step_ref[first + pl.program_id(0)]

        @pl.when(step_ref[2 * count] == 0)
        def _():
            out_ref[step] = found(0, block - skipped)[:half]

        @pl.when(step_ref[2 * count] == 1)
        def _():
            out_ref[step] = found(skipped, block)[half - skipped :]

    whole = pl.BlockSpec((2 * count, half, units), lambda i, step_ref: (0, 0, 0))
    left_specs = [
        pl.BlockSpec((1, x.shape[1], block), lambda i, step_ref: (i // each, 0, i % each)) for x in lefts
    ]
    right_specs = [pl.BlockSpec(x.shape, lambda i, step_ref: (0, 0)) for x in rights]
    return pl.pallas_call(
        kernel,
        grid_spec=pltpu.PrefetchScalarGridSpec(
            num_scalar_prefetch=1,
            grid=(count,),
            in_specs=left_specs + right_specs + [whole] * len(bases),
            out_specs=whole,
        ),
        out_shape=jax.ShapeDtypeStruct((2 * count, half, units), jnp.bfloat16),
        compiler_params=pltpu.CompilerParams(vmem_limit_bytes=24 << 20),
        cost_estimate=cost(
            2 * sum(x.size for x in rights) * halves * part, 2 * sum(x.shape[0] for x in rights) * halves * part
        ),
        name="side_gradient",
    )(steps, *lefts, *rights, *bases)


def after(x, *others):
    return lax.optimization_barrier((x, others))[0]


def received(arrivals):
    pieces, rows, share = arrivals[0].shape

    def kernel(*refs):
        for h, ref in enumerate(refs[:-1]):
            for k in range(pieces):
                refs[-1][h * rows : (h + 1) * rows, k * share : (k + 1) * share] = ref[k].astype(jnp.float32)

    return pl.pallas_call(
        kernel,
        out_shape=jax.ShapeDtypeStruct((rows * len(arrivals), pieces * share), jnp.float32),
        in_specs=in_vmem(len(arrivals)),
        out_specs=pl.BlockSpec(memory_space=pltpu.VMEM),
        compiler_params=pltpu.CompilerParams(vmem_limit_bytes=16 << 20),
        cost_estimate=NO_COST,
        name="received",
    )(*arrivals)


def partner(index, step, count):
    return index ^ step if count & (count - 1) == 0 else (step - index) % count


def shards(tokens, up_weight, down_weight, mod_table, timesteps, valid_counts):
    count, cores, sides = lax.axis_size("dp"), lax.axis_size("mp"), lax.axis_size("side")
    me, core, side = lax.axis_index("dp"), lax.axis_index("mp"), lax.axis_index("side")
    is_student = side == 1
    rows, width = tokens.shape
    pieces = 2 if width % (2 * LANES) == 0 and cores == 2 else 1
    part = width // pieces
    block, hidden = up_weight.shape[1:]
    share = hidden // count
    features = block * count
    first = core * width if cores == 2 else 0
    peers = [partner(me, step, count) for step in range(count)]
    feature_offsets = [(peer * block - first) % features for peer in peers]

    def sent(step, piece):
        pairs = [(i, partner(i, step, count)) for i in range(count)]
        return piece if all(i == j for i, j in pairs) else lax.ppermute(piece, "dp", pairs)

    wide = tokens.astype(jnp.float32)
    own_mean = jnp.mean(wide, axis=-1, keepdims=True)
    own_spread = jnp.sum((wide - own_mean) ** 2, axis=-1, keepdims=True)
    moments = jnp.concatenate([own_mean, own_spread], axis=1)
    if cores == 2:
        all_moments = jnp.stack([moments, from_core(moments, 1)])
    else:
        all_moments = lax.all_gather(moments, "mp")
    average = jnp.mean(all_moments[:, :, :1], axis=0)
    spread = jnp.sum(all_moments[:, :, 1:] + width * (all_moments[:, :, :1] - average) ** 2, axis=0)
    scaled = (wide - average) * lax.rsqrt(spread / features + 1e-06)
    modulation = lax.dynamic_slice(
        mod_table[0], (timesteps[0], 0, core * width), (1, mod_table.shape[2], width)
    )[0]
    normed = (scaled * (1.0 + modulation[1]) + modulation[0]).astype(jnp.bfloat16)
    gate = modulation[2]

    def own_features(array):
        return [ring_gather(array[:, c * part : (c + 1) * part], 1 if c % 2 == 0 else -1) for c in range(pieces)]

    def widened(found):
        own = stacked(found)
        if cores == 2:
            return [own, from_core(own, 1)]
        everything = lax.all_gather(own, "mp")
        return [everything[t] for t in range(cores)]

    def at(t, c):
        start = t * width + c * part
        return slice(start, start + part)

    parts = [(t, c) for t in range(cores) for c in range(pieces)]

    normed_found = own_features(normed)
    ups = [sent(k, lax.dynamic_slice_in_dim(up_weight[0], peers[k] * share, share, 1)) for k in range(count)]
    downs = []
    for k in range(count):
        piece = lax.dynamic_slice_in_dim(down_weight[0], peers[k] * share, share, 0)
        hop = min((k + 1) // 2, (count - 1) // 2)
        if k and hop:
            piece = after(piece, *[found[way] for found in normed_found for way in (hop, count - hop)])
        downs.append(sent(k, piece))
    up = placed_along(0, feature_offsets, ups, features)
    down = placed_along(1, feature_offsets, downs, features)

    all_normed = [widened(found) for found in normed_found]
    hidden_pre = sum(product(all_normed[c][t], up[at(t, c)]) for t, c in parts)
    hidden_act = gelu_tanh(hidden_pre).astype(jnp.bfloat16)

    valid_col = (jnp.arange(rows, dtype=jnp.int32) < valid_counts[me]).astype(jnp.float32)[:, None]
    valid_total = jnp.sum(valid_counts).astype(jnp.float32)

    def of_student(x):
        return jnp.where(is_student, x, lax.ppermute(x, "side", [(1, 0)]))

    student_gate = of_student(gate)
    student_act = of_student(hidden_act)

    outs, grads = [], []
    for c in range(pieces):
        if cores == 2:
            away = product(hidden_act, down[:, at(1, c)]).astype(jnp.bfloat16)
            term = product(hidden_act, down[:, at(0, c)]) + from_core(away, 1).astype(jnp.float32)
        else:
            term = lax.psum_scatter(
                product(hidden_act, down).astype(jnp.bfloat16), "mp", scatter_dimension=1, tiled=True
            ).astype(jnp.float32)
        mixed = ring_scatter([term[r * rows : (r + 1) * rows] for r in range(count)], 1 if c % 2 == 0 else -1)
        own = slice(c * part, (c + 1) * part)
        out = (wide[:, own] + gate[own] * mixed).astype(jnp.bfloat16)
        other = lax.ppermute(out, "side", [(0, 1), (1, 0)])
        differ = out.astype(jnp.float32) - other.astype(jnp.float32)
        differ = jnp.where(is_student, differ, -differ)
        grad = (student_gate[own] * differ * valid_col / jnp.sqrt(valid_total)).astype(jnp.bfloat16)
        outs.append(out)
        grads.append(grad)

    grads_found = lax.optimization_barrier(own_features(jnp.concatenate(grads, axis=1)))
    all_grads = [widened(found) for found in grads_found]

    def over_all_tokens(found, right):
        return jnp.concatenate([over_tokens(found[c][t], right).astype(jnp.bfloat16) for t, c in parts], axis=0)

    taken = block // sides

    def delivered(own):
        own = own.reshape(count * taken, share)
        arrivals = [
            sent(k, lax.dynamic_slice_in_dim(own, feature_offsets[k] // sides, taken, 0)) for k in range(count)
        ]
        result = jnp.zeros((taken, hidden), jnp.float32)
        for peer, piece in zip(peers, arrivals):
            result = lax.dynamic_update_slice_in_dim(result, piece.astype(jnp.float32), peer * share, 1)
        return result

    down_found = over_all_tokens(all_grads, student_act).reshape(count, sides, taken, share)
    down_share = delivered(lax.dynamic_index_in_dim(down_found, side, 1, keepdims=False))
    grad_act = sum(across(all_grads[c][t], down[:, at(t, c)]) for t, c in parts)
    unused, pullback = jax.vjp(gelu_tanh, hidden_pre)
    grad_pre = pullback(grad_act)[0].astype(jnp.bfloat16)
    if cores > 2:
        own_normed, grad_pre = lax.optimization_barrier((normed, grad_pre))
        all_normed = [widened(found) for found in own_features(own_normed)]
    up_found = over_all_tokens(all_normed, grad_pre).reshape(count, sides, taken, share)
    up_share = delivered(jnp.where(is_student, up_found[:, 1], lax.ppermute(up_found[:, 0], "side", [(1, 0)])))
    return (jnp.concatenate(outs, axis=1)[None], up_share, down_share.T)


def paired_shards(tokens, up_weight, down_weight, mod_table, timesteps, valid_counts):
    count = lax.axis_size("dp")
    me, core, side = lax.axis_index("dp"), lax.axis_index("mp"), lax.axis_index("side")
    is_student = side == 1
    rows, width = tokens.shape
    part = width // 2
    block, hidden = up_weight.shape[1:]
    share = hidden // count
    features = block * count
    taken = block // 2
    peers = [partner(me, step, count) for step in range(count)]
    swap = [(0, 1), (1, 0)]

    def feature_offset(owner):
        start = owner * block
        t, c = (start // width + core) % 2, (start // part % 2 + side) % 2
        return (2 * t + c) * part + start % part

    feature_offsets = [feature_offset(peer) for peer in peers]

    def sent(step, piece):
        pairs = [(i, partner(i, step, count)) for i in range(count)]
        return piece if all(i == j for i, j in pairs) else lax.ppermute(piece, "dp", pairs)

    def halves(array):
        return [lax.dynamic_slice_in_dim(array, ((side + c) % 2) * part, part, array.ndim - 1) for c in range(2)]

    def of_student(x):
        return jnp.where(is_student, x, lax.ppermute(x, "side", [(1, 0)]))

    part_places = jnp.stack([(core + t) % 2 * width + (side + c) % 2 * part for t in range(2) for c in range(2)])
    part_places = part_places.astype(jnp.int32)
    gate = lax.dynamic_slice(mod_table[0], (timesteps[0], 2, core * width), (1, 1, width)).reshape(width)
    gates = halves(gate)
    student_gate = of_student(gate)

    farthest = count // 2
    near_images = [0] + [r for hop in range(1, farthest - 1) for r in (hop, count - hop)]
    far_images = [farthest, farthest - 1, farthest + 1]
    steps = jnp.stack([part_places[p] // block + b for p in range(4) for b in range(part // block)])
    steps = jnp.concatenate([steps, side[None].astype(jnp.int32)])

    token_halves = halves(tokens)
    column = lax.broadcasted_iota(jnp.int32, (TILE_ROWS, part), 1)
    digits = jnp.where(column == 0, timesteps[0] % DIGIT, jnp.where(column == 1, timesteps[0] // DIGIT, 0))
    digits = digits.astype(jnp.bfloat16)
    there = back = jnp.concatenate([token_halves[0], digits], axis=0)
    round_ring = [there] + [None] * (count - 1)
    crossed = [jnp.concatenate([token_halves[1], digits], axis=0)]
    table = jnp.pad(mod_table[0], ((0, 0), (0, -mod_table.shape[2] % 8), (0, 0)))

    def cross_over(images):
        return lax.ppermute(stacked([round_ring[r] for r in images]), "side", swap)

    arrived = []
    for hop in range(1, farthest + 1):
        if hop == 2:
            there = after(there, table)
        if hop == farthest:
            there = after(there, crossed[1])
        there = ring_shift(there, 1)
        round_ring[-hop % count] = there
        if hop <= (count - 1) // 2:
            back = ring_shift(back, -1)
            round_ring[hop] = back
        arrived.append([there, back])
        if hop <= farthest - 2:
            crossed.append(cross_over([hop, count - hop]))
    far_crossed = cross_over(far_images)

    def exchanged(x):
        return lax.all_to_all(x, "dp", split_axis=0, concat_axis=0, tiled=True)

    up = exchanged(after(by_columns(up_weight[0], count), *arrived[-1]))
    down_blocks = exchanged(after(down_weight[0], up, crossed, far_crossed))

    def all_features(images, crossed):
        first = stacked([round_ring[r] for r in images])
        steps_taken = first.reshape(len(images), rows + TILE_ROWS, part)[:, rows, :2].astype(jnp.int32)
        pair = [first, crossed]
        shaped = [x.reshape(len(images), rows + TILE_ROWS, part) for x in pair + [from_core(x, 1) for x in pair]]
        return shaped, steps_taken[:, 0] + DIGIT * steps_taken[:, 1]

    near_tokens, near_steps = all_features(near_images, stacked(crossed))
    far_tokens, far_steps = all_features(far_images, far_crossed)
    *far_normed, far_pre, far_act = modulated_up(far_tokens, rows, far_steps, part_places, table, up)
    *near_normed, near_pre, near_act = modulated_up(near_tokens, rows, near_steps, part_places, table, up)

    def down_piece(k):
        return lambda refs, scalar_ref: refs[0].at[k * share : (k + 1) * share, :]

    offsets = [feature_offset(i) for i in range(count)]
    down = placed(1, offsets, [after(down_blocks, near_act, far_act)], [down_piece(k) for k in range(count)], (share, features))

    valid_col = (jnp.arange(rows, dtype=jnp.int32) < valid_counts[me]).astype(jnp.float32)[:, None]
    valid_total = jnp.sum(valid_counts).astype(jnp.float32)
    shares = {}

    def other_share(images, act):
        found = from_core(product(act, down[:, width:]).astype(jnp.bfloat16), 1)
        for k, r in enumerate(images):
            here = slice(k * rows, (k + 1) * rows)
            shares[r] = (act[here], found[here])
        return found

    def term(r, c):
        act, found = shares[r % count]
        here = slice(c * part, (c + 1) * part)
        return product(act, down[:, here]) + found[:, here].astype(jnp.float32)

    ways = (1, -1)
    far_share = other_share(far_images[:1], far_act[:rows])
    there = [ring_shift(term(farthest, c).astype(jnp.bfloat16), ways[c]) for c in range(2)]
    other_share(far_images[1:], after(far_act[rows:], far_share))
    student_act = of_student(jnp.concatenate([near_act, far_act], axis=0))
    back = [None, None]
    other_share(near_images, after(near_act, far_share))
    for hop in range(farthest - 1, 0, -1):
        if hop < farthest - 1:
            there = after(there, back)
        for c in range(2):
            there[c] = term(ways[c] * hop, c) + there[c].astype(jnp.float32)
            there[c] = ring_shift(there[c].astype(jnp.bfloat16), ways[c])
            value = term(-ways[c] * hop, c)
            value = value if back[c] is None else value + back[c].astype(jnp.float32)
            back[c] = ring_shift(value.astype(jnp.bfloat16), -ways[c])
    mixed = [term(0, c) + there[c].astype(jnp.float32) + back[c].astype(jnp.float32) for c in range(2)]
    mixed, student_act = lax.optimization_barrier((mixed, student_act))
    student_acts = [student_act[: len(near_images) * rows], student_act[len(near_images) * rows :]]
    student_gates = halves(student_gate)
    outs = [(token_halves[c].astype(jnp.float32) + gates[c] * mixed[c]).astype(jnp.bfloat16) for c in range(2)]
    found = []
    for c in range(2):
        differ = outs[c].astype(jnp.float32) - lax.ppermute(outs[1 - c], "side", swap).astype(jnp.float32)
        differ = jnp.where(is_student, differ, -differ)
        grad = (student_gates[c] * differ * valid_col / jnp.sqrt(valid_total)).astype(jnp.bfloat16)
        found.append([grad] + [None] * (count - 1))

    there, back = [found[c][0] for c in range(2)], [found[c][0] for c in range(2)]
    for hop in range(1, farthest + 1):
        if hop == 2:
            there = after(there, student_acts)
        if hop == farthest:
            near_own = stacked_parts([[found[c][r] for r in near_images] for c in range(2)])
            near_grads = [near_own, from_core(near_own, 1)]
            there = after(there, near_grads)
        for c, way in ((0, 1), (1, -1)):
            there[c] = ring_shift(there[c], way)
            found[c][(-way * hop) % count] = there[c]
            if hop <= (count - 1) // 2:
                back[c] = ring_shift(back[c], -way)
                found[c][(way * hop) % count] = back[c]
    near_grad_pre = act_gradient(*near_grads, down, near_pre, rows)
    far_found = [[found[c][r] for r in far_images] for c in range(2)]
    near_up = weight_gradient(*near_normed, near_grad_pre, steps, block)
    far_own = stacked_parts(after(far_found, *there, near_up))
    far_grads = [far_own, from_core(far_own, 1)]

    def delivered(found):
        return exchanged(found.reshape(-1, share)).reshape(found.shape)

    own_found = side_gradient([near_grads[0], far_own], student_acts, steps, 0, block)
    far_grads = after(far_grads, own_found)
    far_grad_pre = act_gradient(*far_grads, down, far_pre, rows)
    up_found = weight_gradient(*far_normed, far_grad_pre, steps, block, near_up)
    far_other = after(far_grads[1], up_found)
    down_found = side_gradient([near_grads[1], far_other], student_acts, steps, count // 2, block, own_found)
    down_arrived = delivered(down_found)
    handed = lax.ppermute(up_found[0], "side", [(1, 0)])
    up_arrived = [delivered(jnp.where(is_student, up_found[1], handed))]
    up_share, down_share = received(up_arrived), received([down_arrived])
    out = jnp.concatenate(
        [jnp.where(side == 0, outs[0], outs[1]), jnp.where(side == 0, outs[1], outs[0])], axis=1
    )
    return (out[None], up_share, down_share.T)


def solution(mesh):
    placed = (
        P("dp", "mp"),
        P("side", "dp", "mp"),
        P("side", "mp", "dp"),
        P("side", None, None, None),
        P("dp"),
        P(),
    )
    paired = mesh.shape["mp"] == mesh.shape["side"] == 2 and mesh.shape["dp"] in (8, 16, 32)
    return jax.shard_map(
        paired_shards if paired else shards,
        mesh=mesh,
        in_specs=placed,
        out_specs=(P("side", "dp", "mp"), P(("dp", "side"), "mp"), P("mp", ("dp", "side"))),
        check_vma=False,
    )
```
